256 devices in a mesh: tile: 16 (over x, y_hi, core), trac: 16 (over y_lo, z).
Axes of the slice: x: 4, y: 4 (y_hi: 2, y_lo: 2; y = y_hi * 2 + y_lo), z: 8, core: 2. Of those that a mesh axis runs over, the one named last changes fastest.
Arguments:
- tracers: float32 [128, 4096, 128], P(None, ('tile', 'trac')), may hold values from -6 to 6
- winds: float32 [2, 4096, 128], P(None, ('tile', 'trac')), may hold values from -4 to 4
- chem_linear: float32 [128, 128], replicated, may hold values from -0.5 to 0.5
- chem_loss: float32 [128], replicated, may hold values from 0.5 to 4
- chem_left: float32 [4, 128, 128], replicated, may hold values from -0.25 to 0.25
- chem_right: float32 [4, 128, 128], replicated, may hold values from -0.25 to 0.25
- active_cells: int32 [256], P(('tile', 'trac')), may hold values from 256 to 2048
Outputs:
- tracers_out: float32 [128, 4096, 128], P(None, ('tile', 'trac'))
- winds_out: float32 [2, 4096, 128], P(None, ('tile', 'trac'))
The draws below stay inside these ranges and needn't reach their ends.
Inputs may be any that keep to these rules, and one draw needn't show every extreme that they name: `active_cells`: active cells are the leading ones of the tile in row-major order.
All inputs are finite; a program needn't handle non-finite values.
Results may differ from the reference program's by a relative error of at most 0.0003.
Values sent between devices are 32-bit elements; how exact they have to be, the bound alone decides.
No kernel may reach another device: no remote copies, remote signals or barrier semaphores. Data moves between devices by JAX's collectives and lax.ppermute only.
A program may use at most 64 MiB of HBM per device.

```python
import math
from functools import partial
import jax
import jax.numpy as jnp
from jax import lax

SPECIES = 128
W = 128
SUBS = 4
CHEM_STEPS = 3
PAIRS = 4
TILES = 256
ROWS = 4096
CELLS = 2048


def with_ends(result, rng, smallest, largest):
    extent = result.shape
    spot = [jax.random.randint(jax.random.fold_in(rng, axis), (), 0, extent[axis]) for axis in range(len(extent))]
    result = result.at[tuple(spot)].set(smallest)
    longest = extent.index(max(extent))
    spot[longest] = (spot[longest] + 1) % extent[longest]
    return result.at[tuple(spot)].set(largest)


def levels(own_key, extent, shards, smallest, top_value):
    gain, own = 1.0, jax.random.fold_in(own_key, 6)
    for position, shards_of in shards:
        heights = jnp.exp(jax.random.uniform(jax.random.fold_in(own, position), (shards_of,), jnp.float32, smallest / len(shards), top_value / len(shards)))
        gain = gain * jnp.repeat(heights, extent[position] // shards_of).reshape([-1 if axis == position else 1 for axis in range(len(extent))])
    return gain


def scatter_about(key, dims, scale, reach, pieces=(), kind=jnp.bfloat16):
    entries = jax.random.normal(key, dims, jnp.float32) * scale
    if len(pieces) > 0:
        entries = levels(key, dims, pieces, -0.22, 0.18) * entries
    return jnp.clip(entries, min=-reach, max=reach).astype(kind)


def setup_inputs(seed: int = 0) -> dict:
    seeds = jax.random.split(jax.random.key(seed), 8)
    return {
        "tracers": scatter_about(seeds[0], (SPECIES, ROWS, W), 1.0, 6.0, ((1, 256),), jnp.float32),
        "winds": scatter_about(seeds[1], (2, ROWS, W), 1.0, 4.0, ((1, 256),), jnp.float32),
        "chem_linear": scatter_about(seeds[2], (SPECIES, SPECIES), SPECIES ** -0.5, 0.5, (), jnp.float32),
        "chem_loss": jnp.clip(jnp.exp(jax.random.uniform(seeds[3], (SPECIES,), jnp.float32, math.log(0.5), math.log(4.0))), 0.5, 4.0),
        "chem_left": scatter_about(seeds[4], (PAIRS, SPECIES, SPECIES), (4 * SPECIES) ** -0.5, 0.25, (), jnp.float32),
        "chem_right": scatter_about(seeds[5], (PAIRS, SPECIES, SPECIES), (4 * SPECIES) ** -0.5, 0.25, (), jnp.float32),
        "active_cells": with_ends(jax.random.randint(seeds[6], (TILES,), CELLS // 8, CELLS + 1), jax.random.fold_in(seeds[6], 1), CELLS // 8, CELLS).astype(jnp.int32),
    }


DT_WIND = 0.1
VISCOSITY = 0.2
DT_TRACER = 0.1
DT_CHEM = 0.1


def wrap_rows(field, width):
    return jnp.concatenate([field[:, field.shape[1] - width:, :], field, field[:, :width, :]], axis=1)


def tendency(extended):
    centre = extended[:, 1:-1, :]
    along = (jnp.roll(centre, -1, axis=2) - jnp.roll(centre, 1, axis=2)) * 0.5
    across = (extended[:, 2:, :] - extended[:, :-2, :]) * 0.5
    spread = jnp.roll(centre, -1, axis=2) + jnp.roll(centre, 1, axis=2) + extended[:, 2:, :] + extended[:, :-2, :] - 4.0 * centre
    return -(centre[0:1] * along + centre[1:2] * across) + VISCOSITY * spread


def wind_step(winds, rim):
    first = winds + DT_WIND * tendency(rim(winds))
    second = 0.75 * winds + 0.25 * (first + DT_WIND * tendency(rim(first)))
    return winds / 3.0 + 2.0 / 3.0 * (second + DT_WIND * tendency(rim(second)))


def advect(extended):
    tracer = extended[:-2]
    east = extended[-2, 1:-1, :]
    north = extended[-1]
    centre = tracer[:, 1:-1, :]
    flux = jnp.maximum(east, 0.0) * centre + jnp.minimum(jnp.roll(east, -1, axis=1), 0.0) * jnp.roll(centre, -1, axis=2)
    div_x = flux - jnp.roll(flux, 1, axis=2)
    upward = jnp.maximum(north[:-1], 0.0) * tracer[:, :-1, :] + jnp.minimum(north[1:], 0.0) * tracer[:, 1:, :]
    div_y = upward[:, 1:, :] - upward[:, :-1, :]
    moved = centre - DT_TRACER * (div_x + div_y)
    return jnp.concatenate([moved, extended[-2:, 1:-1, :]], axis=0)


def react(conc, active, linear, loss, both_factors):
    species = conc.shape[0]
    for step in range(CHEM_STEPS):
        rate = jnp.dot(linear, conc, precision=lax.Precision.HIGHEST, preferred_element_type=jnp.float32) - loss[:, None] * conc
        factors = jnp.dot(both_factors, conc, precision=lax.Precision.HIGHEST, preferred_element_type=jnp.float32)
        factors = factors.reshape(2, PAIRS, species, conc.shape[1])
        rate = rate + jnp.sum(factors[0] * factors[1], axis=0)
        conc = conc + DT_CHEM * (rate * active[None, :])
    return conc


def reference(tracers, winds, chem_linear, chem_loss, chem_left, chem_right, active_cells):
    rim = partial(wrap_rows, width=1)
    winds_new = wind_step(winds, rim)
    stretch = math.gcd(SPECIES, 8)
    grouped = tracers.reshape(SPECIES // stretch, stretch, ROWS, W)

    def carry_block(block):
        state = jnp.concatenate([block, winds_new], axis=0)
        for sub in range(SUBS):
            state = advect(rim(state))
        return state[:-2]

    moved = lax.map(carry_block, grouped).reshape(SPECIES, ROWS, W)
    tiled = moved.reshape(SPECIES, TILES, CELLS).transpose(1, 0, 2)
    both_factors = jnp.concatenate([chem_left, chem_right], axis=0).reshape(2 * PAIRS * SPECIES, SPECIES)

    def chem_tile(item):
        conc, count = item
        mask = (jnp.arange(CELLS, dtype=jnp.int32) < count).astype(jnp.float32)
        return react(conc, mask, chem_linear, chem_loss, both_factors)

    done = lax.map(chem_tile, (tiled, active_cells))
    return done.transpose(1, 0, 2).reshape(SPECIES, ROWS, W), winds_new
```

```python
import functools

import jax
import jax.numpy as jnp
from jax import lax
from jax.experimental import pallas as pl
from jax.experimental.pallas import tpu as pltpu
from jax.sharding import PartitionSpec as P

SUBS = 4
CHEM_STEPS = 3
PAIRS = 4
DT_WIND = 0.1
VISCOSITY = 0.2
DT_TRACER = 0.1
DT_CHEM = 0.1

S = 128
R = 16
C = 128
OUTS = S * (1 + 2 * PAIRS)
F32 = jnp.float32
BF16 = jnp.bfloat16
VMEM_LIMIT = 48 * 1024 * 1024


def lanes(x, shift):
    return pltpu.roll(x, shift % C, 1)


def rows_rolled(x, shift):
    return pltpu.roll(x, shift % x.shape[0], 0)


def pack_kernel(x_ref, up_ref, down_ref):
    for r in range(SUBS):
        for g in range(S // 8):
            up_ref[pl.ds(r * S + 8 * g, 8), :] = x_ref[pl.ds(8 * g * R + R - SUBS + r, 8, stride=R), :]
            down_ref[pl.ds(r * S + 8 * g, 8), :] = x_ref[pl.ds(8 * g * R + r, 8, stride=R), :]


def weights_kernel(linear_ref, loss_ref, left_ref, right_ref, w_ref):
    row = lax.broadcasted_iota(jnp.int32, (S, S), 0)
    col = lax.broadcasted_iota(jnp.int32, (S, S), 1)
    diagonal = jnp.where(row == col, jnp.broadcast_to(loss_ref[...], (S, S)), 0.0)
    parts = [linear_ref[...] - diagonal]
    for p in range(PAIRS):
        parts += [left_ref[p], right_ref[p]]
    for i, part in enumerate(parts):
        hi = part.astype(BF16)
        lo = (part - hi.astype(F32)).astype(BF16)
        w_ref[pl.ds(i * S, S), pl.ds(0, S)] = hi
        w_ref[pl.ds(i * S, S), pl.ds(S, S)] = hi
        w_ref[pl.ds(i * S, S), pl.ds(2 * S, S)] = lo
        w_ref[pl.ds(i * S, S), pl.ds(3 * S, S)] = lo


def tendency(u, v):
    out = []
    for f in (u, v):
        east, west, north, south = lanes(f, -1), lanes(f, 1), rows_rolled(f, -1), rows_rolled(f, 1)
        along = (east - west) * 0.5
        across = (north - south) * 0.5
        spread = east + west + north + south - 4.0 * f
        out.append(-(u * along + v * across) + VISCOSITY * spread)
    return out


def wind_step(u, v):
    du, dv = tendency(u, v)
    fu, fv = u + DT_WIND * du, v + DT_WIND * dv
    du, dv = tendency(fu, fv)
    su = 0.75 * u + 0.25 * (fu + DT_WIND * du)
    sv = 0.75 * v + 0.25 * (fv + DT_WIND * dv)
    du, dv = tendency(su, sv)
    return (
        u / 3.0 + 2.0 / 3.0 * (su + DT_WIND * du),
        v / 3.0 + 2.0 / 3.0 * (sv + DT_WIND * dv),
    )


def coefficients(u, v, coef_ref):
    coef_ref[0] = 1.0 - DT_TRACER * (jnp.abs(u) + jnp.abs(v))
    coef_ref[1] = -DT_TRACER * lanes(jnp.minimum(u, 0.0), -1)
    coef_ref[2] = DT_TRACER * lanes(jnp.maximum(u, 0.0), 1)
    coef_ref[3] = -DT_TRACER * rows_rolled(jnp.minimum(v, 0.0), -1)
    coef_ref[4] = DT_TRACER * rows_rolled(jnp.maximum(v, 0.0), 1)


def spread_rows(coef_ref, wide_ref, rows):
    for k in range(5):
        for r in rows:
            wide_ref[k, r] = jnp.broadcast_to(coef_ref[k, pl.ds(r, 1), :], (8, C))


def subcycles(groups, wide_ref, first):
    for sub in range(SUBS):
        size = len(groups[0])
        done = [[] for _ in groups]
        for i in range(1, size - 1):
            k = [wide_ref[j, first + sub + i] for j in range(5)]
            for q, d in zip(groups, done):
                d.append(
                    k[0] * q[i]
                    + k[1] * lanes(q[i], -1)
                    + k[2] * lanes(q[i], 1)
                    + (k[3] * q[i + 1] + k[4] * q[i - 1])
                )
        groups = done
    return groups


def react(conc, scale, w_ref):
    for _ in range(CHEM_STEPS):
        hi = conc.astype(BF16)
        lo = (conc - hi.astype(F32)).astype(BF16)
        both = jnp.concatenate([hi, lo, hi, lo], axis=0)
        y = jnp.dot(w_ref[...], both, preferred_element_type=F32)
        rate = y[0:S]
        for p in range(PAIRS):
            at = (1 + 2 * p) * S
            rate = rate + y[at : at + S] * y[at + S : at + 2 * S]
        conc = conc + rate * scale
    return conc


def scale_of(rows, count):
    col = lax.broadcasted_iota(jnp.int32, (1, C), 1)
    parts = [jnp.where(col + r * C < count, DT_CHEM, 0.0).astype(F32) for r in rows]
    return jnp.concatenate(parts, axis=1)


TOGETHER = 2


def inner_kernel(
    count_ref, x_ref, winds_ref, below_ref, above_ref, w_ref,
    inner_ref, winds_out_ref, wide_winds_ref, coef_ref, wide_ref, conc_ref,
):
    field = [
        jnp.concatenate([below_ref[k, 8:16, :], winds_ref[k], above_ref[k, 0:8, :]], axis=0)
        for k in range(2)
    ]
    u, v = wind_step(*field)
    winds_out_ref[0] = u[8:24]
    winds_out_ref[1] = v[8:24]
    wide_winds_ref[0] = u
    wide_winds_ref[1] = v
    coefficients(u, v, coef_ref)
    spread_rows(coef_ref, wide_ref, range(8 + 1, 8 + R - 1))

    def some_groups(step, carry):
        groups = []
        for k in range(TOGETHER):
            at = (step * TOGETHER + k) * (8 * R)
            groups.append([x_ref[pl.ds(at + r, 8, stride=R), :] for r in range(R)])
        done = subcycles(groups, wide_ref, 8)
        for k in range(TOGETHER):
            at = pl.multiple_of((step * TOGETHER + k) * 8, 8)
            for i, q in enumerate(done[k]):
                conc_ref[i, pl.ds(at, 8), :] = q
        return carry

    lax.fori_loop(0, S // 8 // TOGETHER, some_groups, 0)
    count = count_ref[0]
    for b in range((R - 2 * SUBS) // 2):
        conc = jnp.concatenate([conc_ref[2 * b], conc_ref[2 * b + 1]], axis=1)
        conc = react(conc, scale_of([SUBS + 2 * b, SUBS + 2 * b + 1], count), w_ref)
        inner_ref[2 * b] = conc[:, :C]
        inner_ref[2 * b + 1] = conc[:, C:]


def edge_kernel(
    count_ref, x_ref, below_ref, above_ref, wide_winds_ref, w_ref, inner_ref,
    out_ref, coef_ref, wide_ref, conc_ref,
):
    coefficients(wide_winds_ref[0], wide_winds_ref[1], coef_ref)
    spread_rows(coef_ref, wide_ref, list(range(8 - SUBS + 1, 8 + 2 * SUBS - 1)))
    spread_rows(coef_ref, wide_ref, list(range(8 + R - 2 * SUBS + 1, 8 + R + SUBS - 1)))

    def some_groups(step, carry):
        for side in range(2):
            groups = []
            for k in range(TOGETHER):
                g = step * TOGETHER + k
                own = [
                    x_ref[pl.ds(g * (8 * R) + r + side * (R - 2 * SUBS), 8, stride=R), :]
                    for r in range(2 * SUBS)
                ]
                far_ref = above_ref if side else below_ref
                far = [far_ref[pl.ds(pl.multiple_of(r * S + g * 8, 8), 8), :] for r in range(SUBS)]
                groups.append(own + far if side else far + own)
            done = subcycles(groups, wide_ref, 8 + R - 2 * SUBS if side else 8 - SUBS)
            for k in range(TOGETHER):
                at = pl.multiple_of((step * TOGETHER + k) * 8, 8)
                for i, q in enumerate(done[k]):
                    conc_ref[side * SUBS + i, pl.ds(at, 8), :] = q
        return carry

    lax.fori_loop(0, S // 8 // TOGETHER, some_groups, 0)
    for r in range(R - 2 * SUBS):
        for g in range(S // 8):
            out_ref[pl.ds(8 * g * R + SUBS + r, 8, stride=R), :] = inner_ref[r, pl.ds(8 * g, 8), :]
    count = count_ref[0]
    for b in range(SUBS):
        pair = [r if r < SUBS else R - 2 * SUBS + r for r in (2 * b, 2 * b + 1)]
        conc = jnp.concatenate([conc_ref[2 * b], conc_ref[2 * b + 1]], axis=1)
        conc = react(conc, scale_of(pair, count), w_ref)
        for j, r in enumerate(pair):
            for g in range(S // 8):
                out_ref[pl.ds(8 * g * R + r, 8, stride=R), :] = conc[8 * g : 8 * g + 8, j * C : (j + 1) * C]


def kernel_call(kernel, outs, scratch=(), scalars=0, operands=0):
    vmem = pl.BlockSpec(memory_space=pltpu.VMEM)
    smem = pl.BlockSpec(memory_space=pltpu.SMEM)
    return pl.pallas_call(
        kernel,
        out_shape=[jax.ShapeDtypeStruct(shape, dtype) for shape, dtype in outs],
        in_specs=[smem] * scalars + [vmem] * operands,
        out_specs=[vmem] * len(outs),
        scratch_shapes=[pltpu.VMEM(shape, F32) for shape in scratch],
        compiler_params=pltpu.CompilerParams(vmem_limit_bytes=VMEM_LIMIT),
    )


def on_device(tracers, winds, linear, loss, left, right, active):
    axes = ("tile", "trac")
    size = lax.axis_size(axes)
    up = [(i, (i + 1) % size) for i in range(size)]
    down = [(b, a) for a, b in up]

    winds_below = lax.ppermute(winds, axes, up)
    winds_above = lax.ppermute(winds, axes, down)
    x = tracers.reshape(S * R, C)
    edge = ((SUBS * S, C), F32)
    last, leading = kernel_call(pack_kernel, [edge, edge], operands=1)(x)
    below = lax.ppermute(last, axes, up)
    above = lax.ppermute(leading, axes, down)
    (w,) = kernel_call(weights_kernel, [((OUTS, 4 * S), BF16)], operands=4)(
        linear, loss.reshape(1, S), left, right
    )
    rows = R - 2 * SUBS
    tables = [(5, 32, C), (5, 32, 8, C), (rows, S, C)]
    inner, winds_new, wide_winds = kernel_call(
        inner_kernel,
        [((rows, S, C), F32), ((2, R, C), F32), ((2, 32, C), F32)],
        tables, scalars=1, operands=5,
    )(active, x, winds, winds_below, winds_above, w)
    (out,) = kernel_call(edge_kernel, [((S * R, C), F32)], tables, scalars=1, operands=6)(
        active, x, below, above, wide_winds, w, inner
    )
    return out.reshape(S, R, C), winds_new


def solution(mesh):
    grid = P(None, ("tile", "trac"), None)
    return jax.shard_map(
        on_device,
        mesh=mesh,
        in_specs=(grid, grid, P(), P(), P(), P(), P(("tile", "trac"))),
        out_specs=(grid, grid),
        check_vma=False,
    )
```

```python
import functools

import jax
import jax.numpy as jnp
from jax import lax
from jax.experimental import pallas as pl
from jax.experimental.pallas import tpu as pltpu
from jax.sharding import PartitionSpec as P

SUBS = 4
CHEM_STEPS = 3
PAIRS = 4
DT_WIND = 0.1
VISCOSITY = 0.2
DT_TRACER = 0.1
DT_CHEM = 0.1

AXES = ("tile", "trac")
S = 128
R = 16
C = 128
OUTS = S * (1 + 2 * PAIRS)
F32 = jnp.float32
BF16 = jnp.bfloat16
VMEM_LIMIT = 48 * 1024 * 1024


def lanes(x, shift):
    return pltpu.roll(x, shift % C, 1)


def rows_rolled(x, shift):
    return pltpu.roll(x, shift % x.shape[0], 0)


def is_even():
    return 1 - lax.axis_index(AXES) % 2


def pack_kernel(
    x_hbm, winds_hbm, linear_hbm, loss_hbm, left_hbm, right_hbm,
    near_ref, far_ref, x_ref, winds_ref, raw_ref, loss_ref, sems,
):
    even = is_even()
    moves = []
    for k in range(CHUNKS):
        part = pl.ds(k * (S * R // CHUNKS), S * R // CHUNKS)
        moves.append((x_hbm.at[part], x_ref.at[part]))
    moves.append((winds_hbm, winds_ref))
    moves.append((left_hbm, raw_ref.at[pl.ds(1, PAIRS)]))
    moves.append((right_hbm, raw_ref.at[pl.ds(1 + PAIRS, PAIRS)]))
    moves.append((linear_hbm, raw_ref.at[0]))
    moves.append((loss_hbm, loss_ref))
    copies = [pltpu.make_async_copy(a, b, sems.at[i]) for i, (a, b) in enumerate(moves)]
    for copy in copies:
        copy.start()
    for k in range(CHUNKS):
        copies[k].wait()
        for ref, side in ((near_ref, even), (far_ref, 1 - even)):
            for r in range(SUBS):
                for g in range(k * S // 8 // CHUNKS, (k + 1) * S // 8 // CHUNKS):
                    at = 8 * g * R + r + side * (R - SUBS)
                    ref[pl.ds(r * S + 8 * g, 8), :] = x_ref[pl.ds(at, 8, stride=R), :]
    copies[CHUNKS].wait()
    for ref, side in ((near_ref, even), (far_ref, 1 - even)):
        for k in range(2):
            ref[pl.ds(SUBS * S + 8 * k, 8), :] = winds_ref[k, pl.ds(pl.multiple_of(side * 8, 8), 8), :]
    for copy in copies[CHUNKS + 1 :]:
        copy.wait()


def weights_kernel(raw_ref, loss_ref, w_ref):
    row = lax.broadcasted_iota(jnp.int32, (S, S), 0)
    col = lax.broadcasted_iota(jnp.int32, (S, S), 1)
    diagonal = jnp.where(row == col, jnp.broadcast_to(loss_ref[...], (S, S)), 0.0)
    parts = [raw_ref[0] - diagonal]
    for p in range(PAIRS):
        parts += [raw_ref[1 + p], raw_ref[1 + PAIRS + p]]
    for i, part in enumerate(parts):
        hi = part.astype(BF16)
        lo = (part - hi.astype(F32)).astype(BF16)
        w_ref[pl.ds(i * S, S), pl.ds(0, S)] = hi
        w_ref[pl.ds(i * S, S), pl.ds(S, S)] = hi
        w_ref[pl.ds(i * S, S), pl.ds(2 * S, S)] = lo
        w_ref[pl.ds(i * S, S), pl.ds(3 * S, S)] = lo


def tendency(u, v):
    out = []
    for f in (u, v):
        east, west, north, south = lanes(f, -1), lanes(f, 1), rows_rolled(f, -1), rows_rolled(f, 1)
        along = (east - west) * 0.5
        across = (north - south) * 0.5
        spread = east + west + north + south - 4.0 * f
        out.append(-(u * along + v * across) + VISCOSITY * spread)
    return out


def wind_step(u, v):
    du, dv = tendency(u, v)
    fu, fv = u + DT_WIND * du, v + DT_WIND * dv
    du, dv = tendency(fu, fv)
    su = 0.75 * u + 0.25 * (fu + DT_WIND * du)
    sv = 0.75 * v + 0.25 * (fv + DT_WIND * dv)
    du, dv = tendency(su, sv)
    return (
        u / 3.0 + 2.0 / 3.0 * (su + DT_WIND * du),
        v / 3.0 + 2.0 / 3.0 * (sv + DT_WIND * dv),
    )


def coefficients(u, v, wide_ref, rows):
    tables = [
        1.0 - DT_TRACER * (jnp.abs(u) + jnp.abs(v)),
        -DT_TRACER * lanes(jnp.minimum(u, 0.0), -1),
        DT_TRACER * lanes(jnp.maximum(u, 0.0), 1),
        -DT_TRACER * rows_rolled(jnp.minimum(v, 0.0), -1),
        DT_TRACER * rows_rolled(jnp.maximum(v, 0.0), 1),
    ]
    for k, table in enumerate(tables):
        for i, r in enumerate(rows):
            wide_ref[k, i] = jnp.broadcast_to(table[r : r + 1], (8, C))


def subcycles(groups, wide_ref):
    for sub in range(SUBS):
        size = len(groups[0])
        done = [[] for _ in groups]
        for i in range(1, size - 1):
            k = [wide_ref[j, sub + i - 1] for j in range(5)]
            for q, d in zip(groups, done):
                d.append(
                    k[0] * q[i]
                    + k[1] * lanes(q[i], -1)
                    + k[2] * lanes(q[i], 1)
                    + (k[3] * q[i + 1] + k[4] * q[i - 1])
                )
        groups = done
    return groups


def react(conc, scale, w_ref):
    for _ in range(CHEM_STEPS):
        hi = conc.astype(BF16)
        lo = (conc - hi.astype(F32)).astype(BF16)
        both = jnp.concatenate([hi, lo, hi, lo], axis=0)
        y = jnp.dot(w_ref[...], both, preferred_element_type=F32)
        rate = y[0:S]
        for p in range(PAIRS):
            at = (1 + 2 * p) * S
            rate = rate + y[at : at + S] * y[at + S : at + 2 * S]
        conc = conc + rate * scale
    return conc


TOGETHER = 2
CHUNKS = 4
H = R // 2


def half_kernel(last, *refs):
    (count_ref, x_ref, winds_ref, message_ref, w_ref, *rest) = refs
    if last:
        other_ref, _, out_hbm, winds_out_ref, wide_ref, conc_ref, stage_ref, sem = rest
    else:
        out_hbm, wide_ref, conc_ref, stage_ref, sem = rest
        other_ref = message_ref
    side = 1 - is_even() if last else is_even()
    high = side == 1
    field = []
    for k in range(2):
        here = message_ref[pl.ds(SUBS * S + 8 * k, 8), :]
        there = other_ref[pl.ds(SUBS * S + 8 * k, 8), :]
        field.append(
            jnp.concatenate([jnp.where(high, there, here), winds_ref[k], jnp.where(high, here, there)], axis=0)
        )
    u, v = wind_step(*field)
    if last:
        winds_out_ref[0] = u[8:24]
        winds_out_ref[1] = v[8:24]
    u, v = [jnp.where(high, f[8:32], f[0:24]) for f in (u, v)]
    coefficients(u, v, wide_ref, range(5, 5 + R - 2))

    def some_groups(step, carry):
        groups = []
        for k in range(TOGETHER):
            g = step * TOGETHER + k
            start = g * (8 * R)
            own = [x_ref[pl.ds(start + r + side * SUBS, 8, stride=R), :] for r in range(R - SUBS)]
            halo = [message_ref[pl.ds(pl.multiple_of(r * S + g * 8, 8), 8), :] for r in range(SUBS)]
            groups.append(
                [
                    jnp.where(
                        high,
                        own[i] if i < R - SUBS else halo[i - R + SUBS],
                        halo[i] if i < SUBS else own[i - SUBS],
                    )
                    for i in range(R)
                ]
            )
        done = subcycles(groups, wide_ref)
        for k in range(TOGETHER):
            at = pl.multiple_of((step * TOGETHER + k) * 8, 8)
            for i, q in enumerate(done[k]):
                conc_ref[i, pl.ds(at, 8), :] = q
        return carry

    lax.fori_loop(0, S // 8 // TOGETHER, some_groups, 0)
    conc = jnp.concatenate([conc_ref[i] for i in range(H)], axis=1)
    cell = lax.broadcasted_iota(jnp.int32, (1, H * C), 1) + side * (H * C)
    scale = jnp.where(cell < count_ref[0], DT_CHEM, 0.0).astype(F32)
    conc = react(conc, scale, w_ref)
    flat_ref = stage_ref.reshape(S * H, C)
    for i in range(H):
        for g in range(S // 8):
            flat_ref[pl.ds(8 * g * H + i, 8, stride=H), :] = conc[8 * g : 8 * g + 8, i * C : (i + 1) * C]
    copy = pltpu.make_async_copy(
        stage_ref, out_hbm.at[:, pl.ds(pl.multiple_of(side * H, H), H), :], sem
    )
    copy.start()
    copy.wait()


def on_device(tracers, winds, linear, loss, left, right, active):
    size = lax.axis_size(AXES)
    near = [(i, i ^ 1) for i in range(size)]
    far = [(i, (i + 1 if i % 2 else i - 1) % size) for i in range(size)]

    vmem = pl.BlockSpec(memory_space=pltpu.VMEM)
    smem = pl.BlockSpec(memory_space=pltpu.SMEM)
    hbm = pl.BlockSpec(memory_space=pltpu.HBM)
    params = pltpu.CompilerParams(vmem_limit_bytes=VMEM_LIMIT)
    message = jax.ShapeDtypeStruct((SUBS * S + 16, C), F32)
    to_near, to_far, x, winds, raw, loss = pl.pallas_call(
        pack_kernel,
        out_shape=[
            message,
            message,
            jax.ShapeDtypeStruct((S * R, C), F32),
            jax.ShapeDtypeStruct((2, R, C), F32),
            jax.ShapeDtypeStruct((1 + 2 * PAIRS, S, S), F32),
            jax.ShapeDtypeStruct((1, S), F32),
        ],
        in_specs=[hbm] * 6,
        out_specs=[vmem] * 6,
        scratch_shapes=[pltpu.SemaphoreType.DMA((CHUNKS + 5,))],
        compiler_params=params,
    )(
        *[
            pltpu.with_memory_space_constraint(a, pltpu.HBM)
            for a in (tracers.reshape(S * R, C), winds, linear, loss.reshape(1, S), left, right)
        ]
    )
    from_near = lax.ppermute(to_near, AXES, near)
    from_far = lax.ppermute(to_far, AXES, far)
    w = pl.pallas_call(
        weights_kernel,
        out_shape=jax.ShapeDtypeStruct((OUTS, 4 * S), BF16),
        in_specs=[vmem] * 2,
        out_specs=vmem,
        compiler_params=params,
    )(raw, loss)
    scratch = [
        pltpu.VMEM((5, R - 2, 8, C), F32),
        pltpu.VMEM((H, S, C), F32),
        pltpu.VMEM((S, H, C), F32),
        pltpu.SemaphoreType.DMA,
    ]
    whole = jax.ShapeDtypeStruct((S, R, C), F32)
    half = pl.pallas_call(
        functools.partial(half_kernel, False),
        out_shape=whole,
        in_specs=[smem] + [vmem] * 4,
        out_specs=hbm,
        scratch_shapes=scratch,
        compiler_params=params,
    )(active, x, winds, from_near, w)
    return pl.pallas_call(
        functools.partial(half_kernel, True),
        out_shape=[whole, jax.ShapeDtypeStruct((2, R, C), F32)],
        in_specs=[smem] + [vmem] * 5 + [hbm],
        out_specs=[hbm, vmem],
        scratch_shapes=scratch,
        input_output_aliases={6: 0},
        compiler_params=params,
    )(active, x, winds, from_far, w, from_near, half)


def solution(mesh):
    grid = P(None, ("tile", "trac"), None)
    return jax.shard_map(
        on_device,
        mesh=mesh,
        in_specs=(grid, grid, P(), P(), P(), P(), P(("tile", "trac"))),
        out_specs=(grid, grid),
        check_vma=False,
    )
```

```python
import jax
import jax.numpy as jnp
from jax import lax
from jax.experimental import pallas as pl
from jax.experimental.pallas import tpu as pltpu
from jax.sharding import PartitionSpec as P

SUBS = 4
CHEM_STEPS = 3
PAIRS = 4
DT_WIND = 0.1
VISCOSITY = 0.2
DT_TRACER = 0.1
DT_CHEM = 0.1

AXES = ("tile", "trac")
S = 128
R = 16
C = 128
OUTS = S * (1 + 2 * PAIRS)
F32 = jnp.float32
BF16 = jnp.bfloat16
VMEM_LIMIT = 48 * 1024 * 1024


def lanes(x, shift):
    return pltpu.roll(x, shift % C, 1)


def rows_rolled(x, shift):
    return pltpu.roll(x, shift % x.shape[0], 0)


def is_even():
    return 1 - lax.axis_index(AXES) % 2


def pack_kernel(
    x_hbm, winds_hbm, linear_hbm, loss_hbm, left_hbm, right_hbm,
    near_ref, far_ref, x_ref, winds_ref, raw_ref, loss_ref, sems,
):
    even = is_even()
    moves = []
    for k in range(CHUNKS):
        part = pl.ds(k * (S * R // CHUNKS), S * R // CHUNKS)
        moves.append((x_hbm.at[part], x_ref.at[part]))
    moves.append((winds_hbm, winds_ref))
    moves.append((left_hbm, raw_ref.at[pl.ds(1, PAIRS)]))
    moves.append((right_hbm, raw_ref.at[pl.ds(1 + PAIRS, PAIRS)]))
    moves.append((linear_hbm, raw_ref.at[0]))
    moves.append((loss_hbm, loss_ref))
    copies = [pltpu.make_async_copy(a, b, sems.at[i]) for i, (a, b) in enumerate(moves)]
    for copy in copies:
        copy.start()
    for k in range(CHUNKS):
        copies[k].wait()
        for ref, side in ((near_ref, even), (far_ref, 1 - even)):
            for r in range(SUBS):
                for g in range(k * S // 8 // CHUNKS, (k + 1) * S // 8 // CHUNKS):
                    at = 8 * g * R + r + side * (R - SUBS)
                    ref[pl.ds(r * S + 8 * g, 8), :] = x_ref[pl.ds(at, 8, stride=R), :]
    copies[CHUNKS].wait()
    for ref, side in ((near_ref, even), (far_ref, 1 - even)):
        for k in range(2):
            ref[pl.ds(SUBS * S + 8 * k, 8), :] = winds_ref[k, pl.ds(pl.multiple_of(side * 8, 8), 8), :]
    for copy in copies[CHUNKS + 1 :]:
        copy.wait()


def weights_kernel(count_ref, raw_ref, loss_ref, w_ref, scale_ref):
    cell = lax.broadcasted_iota(jnp.int32, (1, R * C), 1)
    scale_ref[...] = jnp.where(cell < count_ref[0], DT_CHEM, 0.0).astype(F32)
    row = lax.broadcasted_iota(jnp.int32, (S, S), 0)
    col = lax.broadcasted_iota(jnp.int32, (S, S), 1)
    diagonal = jnp.where(row == col, jnp.broadcast_to(loss_ref[...], (S, S)), 0.0)
    parts = [raw_ref[0] - diagonal]
    for p in range(PAIRS):
        parts += [raw_ref[1 + p], raw_ref[1 + PAIRS + p]]
    for i, part in enumerate(parts):
        hi = part.astype(BF16)
        lo = (part - hi.astype(F32)).astype(BF16)
        w_ref[pl.ds(i * S, S), pl.ds(0, S)] = hi
        w_ref[pl.ds(i * S, S), pl.ds(S, S)] = hi
        w_ref[pl.ds(i * S, S), pl.ds(2 * S, S)] = lo
        w_ref[pl.ds(i * S, S), pl.ds(3 * S, S)] = lo


def tendency(u, v):
    out = []
    for f in (u, v):
        east, west, north, south = lanes(f, -1), lanes(f, 1), rows_rolled(f, -1), rows_rolled(f, 1)
        along = (east - west) * 0.5
        across = (north - south) * 0.5
        spread = east + west + north + south - 4.0 * f
        out.append(-(u * along + v * across) + VISCOSITY * spread)
    return out


def wind_step(u, v):
    du, dv = tendency(u, v)
    fu, fv = u + DT_WIND * du, v + DT_WIND * dv
    du, dv = tendency(fu, fv)
    su = 0.75 * u + 0.25 * (fu + DT_WIND * du)
    sv = 0.75 * v + 0.25 * (fv + DT_WIND * dv)
    du, dv = tendency(su, sv)
    return (
        u / 3.0 + 2.0 / 3.0 * (su + DT_WIND * du),
        v / 3.0 + 2.0 / 3.0 * (sv + DT_WIND * dv),
    )


def coefficients(u, v, wide_ref, rows):
    tables = [
        1.0 - DT_TRACER * (jnp.abs(u) + jnp.abs(v)),
        -DT_TRACER * lanes(jnp.minimum(u, 0.0), -1),
        DT_TRACER * lanes(jnp.maximum(u, 0.0), 1),
        -DT_TRACER * rows_rolled(jnp.minimum(v, 0.0), -1),
        DT_TRACER * rows_rolled(jnp.maximum(v, 0.0), 1),
    ]
    for k, table in enumerate(tables):
        for i, r in enumerate(rows):
            wide_ref[k, i] = jnp.broadcast_to(table[r : r + 1], (8, C))


def transport(groups, high, side, x_ref, message_ref, wide_ref, conc_ref):
    states = []
    for g in groups:
        own = [x_ref[pl.ds(g * (8 * R) + r + side * SUBS, 8, stride=R), :] for r in range(R - SUBS)]
        halo = [message_ref[pl.ds(r * S + g * 8, 8), :] for r in range(SUBS)]
        states.append(
            [
                jnp.where(
                    high,
                    own[i] if i < R - SUBS else halo[i - R + SUBS],
                    halo[i] if i < SUBS else own[i - SUBS],
                )
                for i in range(R)
            ]
        )
    for sub in range(SUBS):
        size = len(states[0])
        done = [[] for _ in states]
        for i in range(1, size - 1):
            k = [wide_ref[j, sub + i - 1] for j in range(5)]
            for q, d in zip(states, done):
                d.append(
                    k[0] * q[i]
                    + k[1] * lanes(q[i], -1)
                    + k[2] * lanes(q[i], 1)
                    + (k[3] * q[i + 1] + k[4] * q[i - 1])
                )
        states = done
    for g, q in zip(groups, states):
        for i in range(H):
            conc_ref[i, pl.ds(8 * g, 8), :] = q[i]


def react(conc, scale, w_ref):
    hi = conc.astype(BF16)
    lo = (conc - hi.astype(F32)).astype(BF16)
    both = jnp.concatenate([hi, lo, hi, lo], axis=0)
    y = jnp.dot(w_ref[...], both, preferred_element_type=F32)
    rate = y[0:S]
    for p in range(PAIRS):
        at = (1 + 2 * p) * S
        rate = rate + y[at : at + S] * y[at + S : at + 2 * S]
    return conc + rate * scale


CHUNKS = 4
H = R // 2


def new_winds(winds_ref, lower, upper):
    return wind_step(
        *[jnp.concatenate([lower[k * 8 : k * 8 + 8], winds_ref[k], upper[k * 8 : k * 8 + 8]], axis=0) for k in range(2)]
    )


def half_coefficients(u, v, high, wide_ref):
    u, v = [jnp.where(high, f[8:32], f[0:24]) for f in (u, v)]
    coefficients(u, v, wide_ref, range(5, 5 + R - 2))


def near_kernel(x_ref, winds_ref, message_ref, conc_ref, wide_ref):
    side = is_even()
    high = side == 1
    edge = message_ref[pl.ds(SUBS * S, 16), :]
    u, v = new_winds(winds_ref, edge, edge)
    half_coefficients(u, v, high, wide_ref)
    transport(range(S // 8), high, side, x_ref, message_ref, wide_ref, conc_ref)


def rest_kernel(
    scale_ref, x_ref, winds_ref, near_ref, far_ref, w_ref, near_conc_ref,
    out_hbm, winds_out_ref, wide_ref, conc_ref, stage_ref, sems,
):
    side = 1 - is_even()
    high = side == 1

    def scale_of(side):
        return scale_ref[:, pl.ds(pl.multiple_of(side * (H * C), H * C), H * C)]

    def whole(ref):
        return jnp.concatenate([ref[i] for i in range(H)], axis=1)

    def put(conc, slot, side):
        flat_ref = stage_ref.at[slot].reshape(S * H, C)
        for i in range(H):
            for g in range(S // 8):
                flat_ref[pl.ds(8 * g * H + i, 8, stride=H), :] = conc[8 * g : 8 * g + 8, i * C : (i + 1) * C]
        copy = pltpu.make_async_copy(
            stage_ref.at[slot], out_hbm.at[:, pl.ds(pl.multiple_of(side * H, H), H), :], sems.at[slot]
        )
        copy.start()
        return copy

    near = near_ref[pl.ds(SUBS * S, 16), :]
    far = far_ref[pl.ds(SUBS * S, 16), :]
    u, v = new_winds(winds_ref, jnp.where(high, near, far), jnp.where(high, far, near))
    winds_out_ref[0] = u[8:24]
    winds_out_ref[1] = v[8:24]
    half_coefficients(u, v, high, wide_ref)

    conc = whole(near_conc_ref)
    scale = scale_of(1 - side)
    shares = [range(*b) for b in SHARES]
    for step in range(CHEM_STEPS):
        conc = react(conc, scale, w_ref)
        transport(shares[step], high, side, x_ref, far_ref, wide_ref, conc_ref)
    first = put(conc, 0, 1 - side)
    conc = whole(conc_ref)
    scale = scale_of(side)
    for step in range(CHEM_STEPS):
        conc = react(conc, scale, w_ref)
    second = put(conc, 1, side)
    first.wait()
    second.wait()


SHARES = ((0, 5), (5, 10), (10, 16))


def on_device(tracers, winds, linear, loss, left, right, active):
    size = lax.axis_size(AXES)
    near = [(i, i ^ 1) for i in range(size)]
    far = [(i, (i + 1 if i % 2 else i - 1) % size) for i in range(size)]

    vmem = pl.BlockSpec(memory_space=pltpu.VMEM)
    hbm = pl.BlockSpec(memory_space=pltpu.HBM)
    params = pltpu.CompilerParams(vmem_limit_bytes=VMEM_LIMIT)
    message = jax.ShapeDtypeStruct((SUBS * S + 16, C), F32)
    to_near, to_far, x, winds, raw, loss = pl.pallas_call(
        pack_kernel,
        out_shape=[
            message,
            message,
            jax.ShapeDtypeStruct((S * R, C), F32),
            jax.ShapeDtypeStruct((2, R, C), F32),
            jax.ShapeDtypeStruct((1 + 2 * PAIRS, S, S), F32),
            jax.ShapeDtypeStruct((1, S), F32),
        ],
        in_specs=[hbm] * 6,
        out_specs=[vmem] * 6,
        scratch_shapes=[pltpu.SemaphoreType.DMA((CHUNKS + 5,))],
        compiler_params=params,
    )(
        *[
            pltpu.with_memory_space_constraint(a, pltpu.HBM)
            for a in (tracers.reshape(S * R, C), winds, linear, loss.reshape(1, S), left, right)
        ]
    )
    from_near = lax.ppermute(to_near, AXES, near)
    from_far = lax.ppermute(to_far, AXES, far)
    w, scale = pl.pallas_call(
        weights_kernel,
        out_shape=[jax.ShapeDtypeStruct((OUTS, 4 * S), BF16), jax.ShapeDtypeStruct((1, R * C), F32)],
        in_specs=[pl.BlockSpec(memory_space=pltpu.SMEM), vmem, vmem],
        out_specs=[vmem, vmem],
        compiler_params=params,
    )(active, raw, loss)
    wide = pltpu.VMEM((5, R - 2, 8, C), F32)
    near_conc = pl.pallas_call(
        near_kernel,
        out_shape=jax.ShapeDtypeStruct((H, S, C), F32),
        in_specs=[vmem] * 3,
        out_specs=vmem,
        scratch_shapes=[wide],
        compiler_params=params,
    )(x, winds, from_near)
    return pl.pallas_call(
        rest_kernel,
        out_shape=[jax.ShapeDtypeStruct((S, R, C), F32), jax.ShapeDtypeStruct((2, R, C), F32)],
        in_specs=[vmem] * 7,
        out_specs=[hbm, vmem],
        scratch_shapes=[
            wide,
            pltpu.VMEM((H, S, C), F32),
            pltpu.VMEM((2, S, H, C), F32),
            pltpu.SemaphoreType.DMA((2,)),
        ],
        compiler_params=params,
    )(scale, x, winds, from_near, from_far, w, near_conc)


def solution(mesh):
    grid = P(None, ("tile", "trac"), None)
    return jax.shard_map(
        on_device,
        mesh=mesh,
        in_specs=(grid, grid, P(), P(), P(), P(), P(("tile", "trac"))),
        out_specs=(grid, grid),
        check_vma=False,
    )
```

```python
import jax
import jax.numpy as jnp
from jax import lax
from jax.experimental import pallas as pl
from jax.experimental.pallas import tpu as pltpu
from jax.sharding import PartitionSpec as P

SUBS = 4
CHEM_STEPS = 3
PAIRS = 4
DT_WIND = 0.1
VISCOSITY = 0.2
DT_TRACER = 0.1
DT_CHEM = 0.1

AXES = ("tile", "trac")
S = 128
R = 16
C = 128
OUTS = S * (1 + 2 * PAIRS)
F32 = jnp.float32
BF16 = jnp.bfloat16
VMEM_LIMIT = 48 * 1024 * 1024


def lanes(x, shift):
    return pltpu.roll(x, shift % C, 1)


def rows_rolled(x, shift):
    return pltpu.roll(x, shift % x.shape[0], 0)


def is_even():
    return 1 - lax.axis_index(AXES) % 2


def pack_kernel(
    x_hbm, winds_hbm, linear_hbm, loss_hbm, left_hbm, right_hbm,
    near_ref, far_ref, x_ref, winds_ref, raw_ref, loss_ref, sems,
):
    even = is_even()
    moves = []
    for k in range(CHUNKS):
        part = pl.ds(k * (S * R // CHUNKS), S * R // CHUNKS)
        moves.append((x_hbm.at[part], x_ref.at[part]))
    moves.append((winds_hbm, winds_ref))
    moves.append((left_hbm, raw_ref.at[pl.ds(1, PAIRS)]))
    moves.append((right_hbm, raw_ref.at[pl.ds(1 + PAIRS, PAIRS)]))
    moves.append((linear_hbm, raw_ref.at[0]))
    moves.append((loss_hbm, loss_ref))
    copies = [pltpu.make_async_copy(a, b, sems.at[i]) for i, (a, b) in enumerate(moves)]
    for copy in copies:
        copy.start()
    for k in range(CHUNKS):
        copies[k].wait()
        for ref, side in ((near_ref, even), (far_ref, 1 - even)):
            for r in range(SUBS):
                for g in range(k * S // 8 // CHUNKS, (k + 1) * S // 8 // CHUNKS):
                    at = 8 * g * R + r + side * (R - SUBS)
                    ref[pl.ds(r * S + 8 * g, 8), :] = x_ref[pl.ds(at, 8, stride=R), :]
    copies[CHUNKS].wait()
    for ref, side in ((near_ref, even), (far_ref, 1 - even)):
        for k in range(2):
            ref[pl.ds(SUBS * S + 8 * k, 8), :] = winds_ref[k, pl.ds(pl.multiple_of(side * 8, 8), 8), :]
    for copy in copies[CHUNKS + 1 :]:
        copy.wait()


def weights_kernel(count_ref, raw_ref, loss_ref, w_ref, scale_ref):
    cell = lax.broadcasted_iota(jnp.int32, (1, R * C), 1)
    scale_ref[...] = jnp.where(cell < count_ref[0], DT_CHEM, 0.0).astype(F32)
    row = lax.broadcasted_iota(jnp.int32, (S, S), 0)
    col = lax.broadcasted_iota(jnp.int32, (S, S), 1)
    diagonal = jnp.where(row == col, jnp.broadcast_to(loss_ref[...], (S, S)), 0.0)
    parts = [raw_ref[0] - diagonal]
    for p in range(PAIRS):
        parts += [raw_ref[1 + p], raw_ref[1 + PAIRS + p]]
    for i, part in enumerate(parts):
        hi = part.astype(BF16)
        lo = (part - hi.astype(F32)).astype(BF16)
        w_ref[pl.ds(i * S, S), pl.ds(0, S)] = hi
        w_ref[pl.ds(i * S, S), pl.ds(S, S)] = hi
        w_ref[pl.ds(i * S, S), pl.ds(2 * S, S)] = lo
        w_ref[pl.ds(i * S, S), pl.ds(3 * S, S)] = lo


def tendency(u, v):
    out = []
    for f in (u, v):
        east, west, north, south = lanes(f, -1), lanes(f, 1), rows_rolled(f, -1), rows_rolled(f, 1)
        along = (east - west) * 0.5
        across = (north - south) * 0.5
        spread = east + west + north + south - 4.0 * f
        out.append(-(u * along + v * across) + VISCOSITY * spread)
    return out


def wind_step(u, v):
    du, dv = tendency(u, v)
    fu, fv = u + DT_WIND * du, v + DT_WIND * dv
    du, dv = tendency(fu, fv)
    su = 0.75 * u + 0.25 * (fu + DT_WIND * du)
    sv = 0.75 * v + 0.25 * (fv + DT_WIND * dv)
    du, dv = tendency(su, sv)
    return (
        u / 3.0 + 2.0 / 3.0 * (su + DT_WIND * du),
        v / 3.0 + 2.0 / 3.0 * (sv + DT_WIND * dv),
    )


def coefficients(u, v, wide_ref, rows):
    tables = [
        1.0 - DT_TRACER * (jnp.abs(u) + jnp.abs(v)),
        -DT_TRACER * lanes(jnp.minimum(u, 0.0), -1),
        DT_TRACER * lanes(jnp.maximum(u, 0.0), 1),
        -DT_TRACER * rows_rolled(jnp.minimum(v, 0.0), -1),
        DT_TRACER * rows_rolled(jnp.maximum(v, 0.0), 1),
    ]
    for k, table in enumerate(tables):
        for i, r in enumerate(rows):
            wide_ref[k, i] = jnp.broadcast_to(table[r : r + 1], (8, C))


def transport(groups, high, side, x_ref, message_ref, wide_ref, conc_ref):
    states = []
    for g in groups:
        own = [x_ref[pl.ds(g * (8 * R) + r + side * SUBS, 8, stride=R), :] for r in range(R - SUBS)]
        halo = [message_ref[pl.ds(r * S + g * 8, 8), :] for r in range(SUBS)]
        states.append(
            [
                jnp.where(
                    high,
                    own[i] if i < R - SUBS else halo[i - R + SUBS],
                    halo[i] if i < SUBS else own[i - SUBS],
                )
                for i in range(R)
            ]
        )
    for sub in range(SUBS):
        size = len(states[0])
        done = [[] for _ in states]
        for i in range(1, size - 1):
            k = [wide_ref[j, sub + i - 1] for j in range(5)]
            for q, d in zip(states, done):
                d.append(
                    k[0] * q[i]
                    + k[1] * lanes(q[i], -1)
                    + k[2] * lanes(q[i], 1)
                    + (k[3] * q[i + 1] + k[4] * q[i - 1])
                )
        states = done
    for g, q in zip(groups, states):
        for i in range(H):
            conc_ref[i, pl.ds(8 * g, 8), :] = q[i]


def react(conc, scale, w_ref):
    hi = conc.astype(BF16)
    lo = (conc - hi.astype(F32)).astype(BF16)
    both = jnp.concatenate([hi, lo, hi, lo], axis=0)
    y = jnp.dot(w_ref[...], both, preferred_element_type=F32)
    rate = y[0:S]
    for p in range(PAIRS):
        at = (1 + 2 * p) * S
        rate = rate + y[at : at + S] * y[at + S : at + 2 * S]
    return conc + rate * scale


CHUNKS = 4
H = R // 2


def scale_of(scale_ref, side):
    return scale_ref[:, pl.ds(pl.multiple_of(side * (H * C), H * C), H * C)]


def whole(ref):
    return jnp.concatenate([ref[i] for i in range(H)], axis=1)


def new_winds(winds_ref, lower, upper):
    return wind_step(
        *[jnp.concatenate([lower[k * 8 : k * 8 + 8], winds_ref[k], upper[k * 8 : k * 8 + 8]], axis=0) for k in range(2)]
    )


def half_coefficients(u, v, high, wide_ref):
    u, v = [jnp.where(high, f[8:32], f[0:24]) for f in (u, v)]
    coefficients(u, v, wide_ref, range(5, 5 + R - 2))


def near_kernel(scale_ref, x_ref, winds_ref, message_ref, w_ref, out_ref, wide_ref, conc_ref):
    side = is_even()
    high = side == 1
    edge = message_ref[pl.ds(SUBS * S, 16), :]
    u, v = new_winds(winds_ref, edge, edge)
    half_coefficients(u, v, high, wide_ref)
    transport(range(S // 8), high, side, x_ref, message_ref, wide_ref, conc_ref)
    conc = whole(conc_ref)
    for _ in range(NEAR_STEPS):
        conc = react(conc, scale_of(scale_ref, side), w_ref)
    for i in range(H):
        out_ref[i] = conc[:, i * C : (i + 1) * C]


def rest_kernel(
    scale_ref, x_ref, winds_ref, near_ref, far_ref, w_ref, near_conc_ref,
    out_hbm, winds_out_ref, wide_ref, conc_ref, stage_ref, sems,
):
    side = 1 - is_even()
    high = side == 1

    def put(conc, slot, side):
        flat_ref = stage_ref.at[slot].reshape(S * H, C)
        for i in range(H):
            for g in range(S // 8):
                flat_ref[pl.ds(8 * g * H + i, 8, stride=H), :] = conc[8 * g : 8 * g + 8, i * C : (i + 1) * C]
        copy = pltpu.make_async_copy(
            stage_ref.at[slot], out_hbm.at[:, pl.ds(pl.multiple_of(side * H, H), H), :], sems.at[slot]
        )
        copy.start()
        return copy

    near = near_ref[pl.ds(SUBS * S, 16), :]
    far = far_ref[pl.ds(SUBS * S, 16), :]
    u, v = new_winds(winds_ref, jnp.where(high, near, far), jnp.where(high, far, near))
    winds_out_ref[0] = u[8:24]
    winds_out_ref[1] = v[8:24]
    half_coefficients(u, v, high, wide_ref)

    conc = whole(near_conc_ref)
    scale = scale_of(scale_ref, 1 - side)
    for share in SHARES:
        conc = react(conc, scale, w_ref)
        transport(range(*share), high, side, x_ref, far_ref, wide_ref, conc_ref)
    first = put(conc, 0, 1 - side)
    conc = whole(conc_ref)
    scale = scale_of(scale_ref, side)
    for step in range(CHEM_STEPS):
        conc = react(conc, scale, w_ref)
    second = put(conc, 1, side)
    first.wait()
    second.wait()


NEAR_STEPS = 2
SHARES = ((0, 16),)


def on_device(tracers, winds, linear, loss, left, right, active):
    size = lax.axis_size(AXES)
    near = [(i, i ^ 1) for i in range(size)]
    far = [(i, (i + 1 if i % 2 else i - 1) % size) for i in range(size)]

    vmem = pl.BlockSpec(memory_space=pltpu.VMEM)
    hbm = pl.BlockSpec(memory_space=pltpu.HBM)
    params = pltpu.CompilerParams(vmem_limit_bytes=VMEM_LIMIT)
    message = jax.ShapeDtypeStruct((SUBS * S + 16, C), F32)
    to_near, to_far, x, winds, raw, loss = pl.pallas_call(
        pack_kernel,
        out_shape=[
            message,
            message,
            jax.ShapeDtypeStruct((S * R, C), F32),
            jax.ShapeDtypeStruct((2, R, C), F32),
            jax.ShapeDtypeStruct((1 + 2 * PAIRS, S, S), F32),
            jax.ShapeDtypeStruct((1, S), F32),
        ],
        in_specs=[hbm] * 6,
        out_specs=[vmem] * 6,
        scratch_shapes=[pltpu.SemaphoreType.DMA((CHUNKS + 5,))],
        compiler_params=params,
    )(
        *[
            pltpu.with_memory_space_constraint(a, pltpu.HBM)
            for a in (tracers.reshape(S * R, C), winds, linear, loss.reshape(1, S), left, right)
        ]
    )
    from_near = lax.ppermute(to_near, AXES, near)
    from_far = lax.ppermute(to_far, AXES, far)
    w, scale = pl.pallas_call(
        weights_kernel,
        out_shape=[jax.ShapeDtypeStruct((OUTS, 4 * S), BF16), jax.ShapeDtypeStruct((1, R * C), F32)],
        in_specs=[pl.BlockSpec(memory_space=pltpu.SMEM), vmem, vmem],
        out_specs=[vmem, vmem],
        compiler_params=params,
    )(active, raw, loss)
    wide = pltpu.VMEM((5, R - 2, 8, C), F32)
    near_conc = pl.pallas_call(
        near_kernel,
        out_shape=jax.ShapeDtypeStruct((H, S, C), F32),
        in_specs=[vmem] * 5,
        out_specs=vmem,
        scratch_shapes=[wide, pltpu.VMEM((H, S, C), F32)],
        compiler_params=params,
    )(scale, x, winds, from_near, w)
    return pl.pallas_call(
        rest_kernel,
        out_shape=[jax.ShapeDtypeStruct((S, R, C), F32), jax.ShapeDtypeStruct((2, R, C), F32)],
        in_specs=[vmem] * 7,
        out_specs=[hbm, vmem],
        scratch_shapes=[
            wide,
            pltpu.VMEM((H, S, C), F32),
            pltpu.VMEM((2, S, H, C), F32),
            pltpu.SemaphoreType.DMA((2,)),
        ],
        compiler_params=params,
    )(scale, x, winds, from_near, from_far, w, near_conc)


def solution(mesh):
    grid = P(None, ("tile", "trac"), None)
    return jax.shard_map(
        on_device,
        mesh=mesh,
        in_specs=(grid, grid, P(), P(), P(), P(), P(("tile", "trac"))),
        out_specs=(grid, grid),
        check_vma=False,
    )
```

```python
import functools

import jax
import jax.numpy as jnp
from jax import lax
from jax.experimental import pallas as pl
from jax.experimental.pallas import tpu as pltpu
from jax.sharding import PartitionSpec as P

SUBS = 4
CHEM_STEPS = 3
PAIRS = 4
DT_WIND = 0.1
VISCOSITY = 0.2
DT_TRACER = 0.1
DT_CHEM = 0.1

AXES = ("tile", "trac")
RUN = 8
S = 128
R = 16
C = 128
OUTS = S * (1 + 2 * PAIRS)
F32 = jnp.float32
BF16 = jnp.bfloat16
VMEM_LIMIT = 48 * 1024 * 1024


def lanes(x, shift):
    return pltpu.roll(x, shift % C, 1)


def rows_rolled(x, shift):
    return pltpu.roll(x, shift % x.shape[0], 0)


def is_even():
    return 1 - lax.axis_index(AXES) % 2


def far_part(far_refs, at, size):
    late = lax.axis_index(AXES) % RUN == RUN - 1
    return jnp.where(late, far_refs[1][pl.ds(at, size), :], far_refs[0][pl.ds(at, size), :])


def pack_kernel(
    x_hbm, winds_hbm, linear_hbm, loss_hbm, left_hbm, right_hbm,
    near_ref, far_ref, x_ref, winds_ref, raw_ref, loss_ref, sems,
):
    even = is_even()
    moves = []
    for k in range(CHUNKS):
        part = pl.ds(k * (S * R // CHUNKS), S * R // CHUNKS)
        moves.append((x_hbm.at[part], x_ref.at[part]))
    moves.append((winds_hbm, winds_ref))
    moves.append((left_hbm, raw_ref.at[pl.ds(1, PAIRS)]))
    moves.append((right_hbm, raw_ref.at[pl.ds(1 + PAIRS, PAIRS)]))
    moves.append((linear_hbm, raw_ref.at[0]))
    moves.append((loss_hbm, loss_ref))
    copies = [pltpu.make_async_copy(a, b, sems.at[i]) for i, (a, b) in enumerate(moves)]
    for copy in copies:
        copy.start()
    for k in range(CHUNKS):
        copies[k].wait()
        for ref, side in ((near_ref, even), (far_ref, 1 - even)):
            for r in range(SUBS):
                for g in range(k * S // 8 // CHUNKS, (k + 1) * S // 8 // CHUNKS):
                    at = 8 * g * R + r + side * (R - SUBS)
                    ref[pl.ds(r * S + 8 * g, 8), :] = x_ref[pl.ds(at, 8, stride=R), :]
    copies[CHUNKS].wait()
    for ref, side in ((near_ref, even), (far_ref, 1 - even)):
        for k in range(2):
            ref[pl.ds(SUBS * S + 8 * k, 8), :] = winds_ref[k, pl.ds(pl.multiple_of(side * 8, 8), 8), :]
    for copy in copies[CHUNKS + 1 :]:
        copy.wait()


def weights_kernel(raw_ref, loss_ref, w_ref):
    row = lax.broadcasted_iota(jnp.int32, (S, S), 0)
    col = lax.broadcasted_iota(jnp.int32, (S, S), 1)
    diagonal = jnp.where(row == col, jnp.broadcast_to(loss_ref[...], (S, S)), 0.0)
    parts = [raw_ref[0] - diagonal]
    for p in range(PAIRS):
        parts += [raw_ref[1 + p], raw_ref[1 + PAIRS + p]]
    for i, part in enumerate(parts):
        hi = part.astype(BF16)
        lo = (part - hi.astype(F32)).astype(BF16)
        w_ref[pl.ds(i * S, S), pl.ds(0, S)] = hi
        w_ref[pl.ds(i * S, S), pl.ds(S, S)] = hi
        w_ref[pl.ds(i * S, S), pl.ds(2 * S, S)] = lo
        w_ref[pl.ds(i * S, S), pl.ds(3 * S, S)] = lo


def tendency(u, v):
    out = []
    for f in (u, v):
        east, west, north, south = lanes(f, -1), lanes(f, 1), rows_rolled(f, -1), rows_rolled(f, 1)
        along = (east - west) * 0.5
        across = (north - south) * 0.5
        spread = east + west + north + south - 4.0 * f
        out.append(-(u * along + v * across) + VISCOSITY * spread)
    return out


def wind_step(u, v):
    du, dv = tendency(u, v)
    fu, fv = u + DT_WIND * du, v + DT_WIND * dv
    du, dv = tendency(fu, fv)
    su = 0.75 * u + 0.25 * (fu + DT_WIND * du)
    sv = 0.75 * v + 0.25 * (fv + DT_WIND * dv)
    du, dv = tendency(su, sv)
    return (
        u / 3.0 + 2.0 / 3.0 * (su + DT_WIND * du),
        v / 3.0 + 2.0 / 3.0 * (sv + DT_WIND * dv),
    )


def row_of(m):
    return is_even() * (R - 1 - 2 * m) + m


def near_row(m):
    return is_even() * (-1 - m) + (1 - is_even()) * (m + SUBS)


def far_row(m):
    return is_even() * (R + SUBS - 1 - m) + (1 - is_even()) * (m - R)


def coefficients(u, v, coef_ref, wide_ref, ms):
    north = -DT_TRACER * rows_rolled(jnp.minimum(v, 0.0), -1)
    south = DT_TRACER * rows_rolled(jnp.maximum(v, 0.0), 1)
    even = is_even() == 1
    coef_ref[0] = 1.0 - DT_TRACER * (jnp.abs(u) + jnp.abs(v))
    coef_ref[1] = -DT_TRACER * lanes(jnp.minimum(u, 0.0), -1)
    coef_ref[2] = DT_TRACER * lanes(jnp.maximum(u, 0.0), 1)
    coef_ref[3] = jnp.where(even, south, north)
    coef_ref[4] = jnp.where(even, north, south)
    for i, m in enumerate(ms):
        for k in range(5):
            wide_ref[k, i] = jnp.broadcast_to(coef_ref[k, pl.ds(row_of(m) + 8, 1), :], (8, C))


def subcycle(states, ms, wide_ref, first):
    done = {}
    for m in ms:
        k = [wide_ref[j, m - first] for j in range(5)]
        done[m] = [
            k[0] * q + k[1] * lanes(q, -1) + k[2] * lanes(q, 1) + (k[3] * above + k[4] * below)
            for q, above, below in zip(states[m], states[m + 1], states[m - 1])
        ]
    return done


def own_rows(x_ref, ms):
    return {m: [x_ref[pl.ds(8 * g * R + row_of(m), 8, stride=R), :] for g in range(S // 8)] for m in ms}


def stored(ref, slot):
    return [ref[slot, pl.ds(8 * g, 8), :] for g in range(S // 8)]


def store(ref, slot, groups):
    for g, q in enumerate(groups):
        ref[slot, pl.ds(8 * g, 8), :] = q


def halo_rows(part, ms, place):
    return {m: [part(pl.multiple_of(place(m) * S + 8 * g, 8), 8) for g in range(S // 8)] for m in ms}


def react(conc, scale, w_ref):
    hi = conc.astype(BF16)
    lo = (conc - hi.astype(F32)).astype(BF16)
    both = jnp.concatenate([hi, lo, hi, lo], axis=0)
    y = jnp.dot(w_ref[...], both, preferred_element_type=F32)
    rate = y[0:S]
    for p in range(PAIRS):
        at = (1 + 2 * p) * S
        rate = rate + y[at : at + S] * y[at + S : at + 2 * S]
    return conc + rate * scale


CHUNKS = 4
H = R // 2


def scale_of(count_ref, ms):
    col = lax.broadcasted_iota(jnp.int32, (1, C), 1)
    return jnp.concatenate(
        [jnp.where(col + row_of(m) * C < count_ref[0], DT_CHEM, 0.0).astype(F32) for m in ms], axis=1
    )


def whole(ref, slots):
    return jnp.concatenate([ref[i] for i in slots], axis=1)


def new_winds(winds_ref, near_part, far_part):
    even = is_even() == 1
    field = []
    for k in range(2):
        near = near_part(SUBS * S + 8 * k, 8)
        far = far_part(SUBS * S + 8 * k, 8)
        field.append(
            jnp.concatenate([jnp.where(even, far, near), winds_ref[k], jnp.where(even, near, far)], axis=0)
        )
    return wind_step(*field)


def part_of(ref, at, size):
    return ref[pl.ds(at, size), :]


FAR_FIRST = R - SUBS
SAVED = 2 * (SUBS - 1) + 1


def near_kernel(count_ref, x_ref, winds_ref, near_ref, w_ref, conc_ref, saved_ref, coef_ref, wide_ref):
    near = functools.partial(part_of, near_ref)
    u, v = new_winds(winds_ref, near, near)
    coefficients(u, v, coef_ref, wide_ref, range(1 - SUBS, FAR_FIRST))
    states = own_rows(x_ref, range(FAR_FIRST + 1)) | halo_rows(near, range(-SUBS, 0), near_row)
    for sub in range(SUBS):
        states = subcycle(states, range(1 - SUBS + sub, FAR_FIRST - sub), wide_ref, 1 - SUBS)
        last = FAR_FIRST - sub - 1
        if sub < SUBS - 1:
            store(saved_ref, 2 * sub, states[last - 1])
            store(saved_ref, 2 * sub + 1, states[last])
        else:
            store(saved_ref, 2 * sub, states[last])
    for m in range(H):
        store(conc_ref, m, states[m])
    conc = whole(conc_ref, range(H))
    for _ in range(NEAR_STEPS):
        conc = react(conc, scale_of(count_ref, range(H)), w_ref)
    for m in range(H):
        conc_ref[m] = conc[:, m * C : (m + 1) * C]


def far_transport(x_ref, far, saved_ref, wide_ref, conc_ref):
    states = own_rows(x_ref, range(FAR_FIRST - 1, R)) | halo_rows(far, range(R, R + SUBS), far_row)
    for sub in range(SUBS):
        first = FAR_FIRST - sub
        states = subcycle(states, range(first, first + H - 1), wide_ref, FAR_FIRST - SUBS + 1)
        if sub < SUBS - 1:
            states[first - 2] = stored(saved_ref, 2 * sub)
            states[first - 1] = stored(saved_ref, 2 * sub + 1)
    store(conc_ref, 0, stored(saved_ref, SAVED - 1))
    for m in range(H + 1, R):
        store(conc_ref, m - H, states[m])


def rest_kernel(
    count_ref, x_ref, winds_ref, near_ref, late_ref, far_ref, w_ref, near_conc_ref, saved_ref,
    out_hbm, winds_out_ref, coef_ref, wide_ref, conc_ref, stage_ref, sems,
):
    def put(conc, slot, high):
        flat_ref = stage_ref.at[slot].reshape(S * H, C)
        for i in range(H):
            at = is_even() * (H - 1 - 2 * i) + i
            for g in range(S // 8):
                flat_ref[pl.ds(8 * g * H + at, 8, stride=H), :] = conc[8 * g : 8 * g + 8, i * C : (i + 1) * C]
        copy = pltpu.make_async_copy(
            stage_ref.at[slot], out_hbm.at[:, pl.ds(pl.multiple_of(high * H, H), H), :], sems.at[slot]
        )
        copy.start()
        return copy

    far = functools.partial(far_part, (far_ref, late_ref))
    u, v = new_winds(winds_ref, functools.partial(part_of, near_ref), far)
    winds_out_ref[0] = u[8:24]
    winds_out_ref[1] = v[8:24]
    coefficients(u, v, coef_ref, wide_ref, range(FAR_FIRST - SUBS + 1, R + SUBS - 1))
    conc = whole(near_conc_ref, range(H))
    for step in range(NEAR_STEPS, CHEM_STEPS):
        conc = react(conc, scale_of(count_ref, range(H)), w_ref)
    first = put(conc, 0, is_even())
    far_transport(x_ref, far, saved_ref, wide_ref, conc_ref)
    conc = whole(conc_ref, range(H))
    for step in range(CHEM_STEPS):
        conc = react(conc, scale_of(count_ref, range(H, R)), w_ref)
    second = put(conc, 1, 1 - is_even())
    first.wait()
    second.wait()


NEAR_STEPS = 2


def on_device(tracers, winds, linear, loss, left, right, active):
    size = lax.axis_size(AXES)
    near = [(i, i ^ 1) for i in range(size)]
    up = [(i, (i + 1) % size) for i in range(1, size, 2)]
    late = [(b, a) for a, b in up if a % RUN == RUN - 1]
    far = up + [(b, a) for a, b in up if a % RUN != RUN - 1]
    smem = pl.BlockSpec(memory_space=pltpu.SMEM)
    vmem = pl.BlockSpec(memory_space=pltpu.VMEM)
    hbm = pl.BlockSpec(memory_space=pltpu.HBM)
    params = pltpu.CompilerParams(vmem_limit_bytes=VMEM_LIMIT)
    message = jax.ShapeDtypeStruct((SUBS * S + 16, C), F32)
    to_near, to_far, x, winds, raw, loss = pl.pallas_call(
        pack_kernel,
        out_shape=[
            message,
            message,
            jax.ShapeDtypeStruct((S * R, C), F32),
            jax.ShapeDtypeStruct((2, R, C), F32),
            jax.ShapeDtypeStruct((1 + 2 * PAIRS, S, S), F32),
            jax.ShapeDtypeStruct((1, S), F32),
        ],
        in_specs=[hbm] * 6,
        out_specs=[vmem] * 6,
        scratch_shapes=[pltpu.SemaphoreType.DMA((CHUNKS + 5,))],
        compiler_params=params,
    )(
        *[
            pltpu.with_memory_space_constraint(a, pltpu.HBM)
            for a in (tracers.reshape(S * R, C), winds, linear, loss.reshape(1, S), left, right)
        ]
    )
    from_near = lax.ppermute(to_near, AXES, near)
    from_far = lax.ppermute(to_far, AXES, far)
    from_late = lax.ppermute(to_far, AXES, late)
    w = pl.pallas_call(
        weights_kernel,
        out_shape=jax.ShapeDtypeStruct((OUTS, 4 * S), BF16),
        in_specs=[vmem] * 2,
        out_specs=vmem,
        compiler_params=params,
    )(raw, loss)
    coef = pltpu.VMEM((5, R + 16, C), F32)
    half = jax.ShapeDtypeStruct((H, S, C), F32)
    conc, saved = pl.pallas_call(
        near_kernel,
        out_shape=[half, jax.ShapeDtypeStruct((SAVED, S, C), F32)],
        in_specs=[smem] + [vmem] * 4,
        out_specs=[vmem] * 2,
        scratch_shapes=[coef, pltpu.VMEM((5, FAR_FIRST + SUBS - 1, 8, C), F32)],
        compiler_params=params,
    )(active, x, winds, from_near, w)
    return pl.pallas_call(
        rest_kernel,
        out_shape=[jax.ShapeDtypeStruct((S, R, C), F32), jax.ShapeDtypeStruct((2, R, C), F32)],
        in_specs=[smem] + [vmem] * 8,
        out_specs=[hbm, vmem],
        scratch_shapes=[
            coef,
            pltpu.VMEM((5, H + SUBS - 2, 8, C), F32),
            pltpu.VMEM((H, S, C), F32),
            pltpu.VMEM((2, S, H, C), F32),
            pltpu.SemaphoreType.DMA((2,)),
        ],
        compiler_params=params,
    )(active, x, winds, from_near, from_late, from_far, w, conc, saved)


def solution(mesh):
    grid = P(None, ("tile", "trac"), None)
    return jax.shard_map(
        on_device,
        mesh=mesh,
        in_specs=(grid, grid, P(), P(), P(), P(), P(("tile", "trac"))),
        out_specs=(grid, grid),
        check_vma=False,
    )
```

```python
import jax
import jax.numpy as jnp
from jax import lax
from jax.experimental import pallas as pl
from jax.experimental.pallas import tpu as pltpu
from jax.sharding import PartitionSpec as P

SUBS = 4
CHEM_STEPS = 3
PAIRS = 4
DT_WIND = 0.1
VISCOSITY = 0.2
DT_TRACER = 0.1
DT_CHEM = 0.1

AXES = ("tile", "trac")
S = 128
R = 16
C = 128
OUTS = S * (1 + 2 * PAIRS)
F32 = jnp.float32
BF16 = jnp.bfloat16
VMEM_LIMIT = 48 * 1024 * 1024


def lanes(x, shift):
    return pltpu.roll(x, shift % C, 1)


def rows_rolled(x, shift):
    return pltpu.roll(x, shift % x.shape[0], 0)


def is_even():
    return 1 - lax.axis_index(AXES) % 2


def pack_kernel(
    x_hbm, winds_hbm, linear_hbm, loss_hbm, left_hbm, right_hbm,
    near_ref, far_ref, x_ref, winds_ref, raw_ref, loss_ref, sems,
):
    even = is_even()
    moves = []
    for k in range(CHUNKS):
        part = pl.ds(k * (S * R // CHUNKS), S * R // CHUNKS)
        moves.append((x_hbm.at[part], x_ref.at[part]))
    moves.append((winds_hbm, winds_ref))
    moves.append((left_hbm, raw_ref.at[pl.ds(1, PAIRS)]))
    moves.append((right_hbm, raw_ref.at[pl.ds(1 + PAIRS, PAIRS)]))
    moves.append((linear_hbm, raw_ref.at[0]))
    moves.append((loss_hbm, loss_ref))
    copies = [pltpu.make_async_copy(a, b, sems.at[i]) for i, (a, b) in enumerate(moves)]
    for copy in copies:
        copy.start()
    for k in range(CHUNKS):
        copies[k].wait()
        for ref, side in ((near_ref, even), (far_ref, 1 - even)):
            for r in range(SUBS):
                for g in range(k * S // 8 // CHUNKS, (k + 1) * S // 8 // CHUNKS):
                    at = 8 * g * R + r + side * (R - SUBS)
                    ref[pl.ds(r * S + 8 * g, 8), :] = x_ref[pl.ds(at, 8, stride=R), :]
    copies[CHUNKS].wait()
    for ref, side in ((near_ref, even), (far_ref, 1 - even)):
        for k in range(2):
            ref[pl.ds(SUBS * S + 8 * k, 8), :] = winds_ref[k, pl.ds(pl.multiple_of(side * 8, 8), 8), :]
    for copy in copies[CHUNKS + 1 :]:
        copy.wait()


def weights_kernel(count_ref, raw_ref, loss_ref, w_ref, scale_ref):
    cell = lax.broadcasted_iota(jnp.int32, (R, C), 0) * C + lax.broadcasted_iota(jnp.int32, (R, C), 1)
    scale_ref[...] = jnp.where(cell < count_ref[0], DT_CHEM, 0.0).astype(F32)
    row = lax.broadcasted_iota(jnp.int32, (S, S), 0)
    col = lax.broadcasted_iota(jnp.int32, (S, S), 1)
    diagonal = jnp.where(row == col, jnp.broadcast_to(loss_ref[...], (S, S)), 0.0)
    parts = [raw_ref[0] - diagonal]
    for p in range(PAIRS):
        parts += [raw_ref[1 + p], raw_ref[1 + PAIRS + p]]
    for i, part in enumerate(parts):
        hi = part.astype(BF16)
        lo = (part - hi.astype(F32)).astype(BF16)
        for c in range(S // B):
            rows = pl.ds((c * len(parts) + i) * B, B)
            for k, piece in enumerate((hi, hi, lo, lo)):
                w_ref[rows, pl.ds(k * S, S)] = piece[c * B : (c + 1) * B]


def tendency(u, v):
    out = []
    for f in (u, v):
        east, west, north, south = lanes(f, -1), lanes(f, 1), rows_rolled(f, -1), rows_rolled(f, 1)
        along = (east - west) * 0.5
        across = (north - south) * 0.5
        spread = east + west + north + south - 4.0 * f
        out.append(-(u * along + v * across) + VISCOSITY * spread)
    return out


def wind_step(u, v):
    du, dv = tendency(u, v)
    fu, fv = u + DT_WIND * du, v + DT_WIND * dv
    du, dv = tendency(fu, fv)
    su = 0.75 * u + 0.25 * (fu + DT_WIND * du)
    sv = 0.75 * v + 0.25 * (fv + DT_WIND * dv)
    du, dv = tendency(su, sv)
    return (
        u / 3.0 + 2.0 / 3.0 * (su + DT_WIND * du),
        v / 3.0 + 2.0 / 3.0 * (sv + DT_WIND * dv),
    )


def row_of(m):
    return is_even() * (R - 1 - 2 * m) + m


def near_row(m):
    return is_even() * (-1 - m) + (1 - is_even()) * (m + SUBS)


def far_row(m):
    return is_even() * (R + SUBS - 1 - m) + (1 - is_even()) * (m - R)


def coefficients(u, v, coef_ref, wide_ref, ms):
    north = -DT_TRACER * rows_rolled(jnp.minimum(v, 0.0), -1)
    south = DT_TRACER * rows_rolled(jnp.maximum(v, 0.0), 1)
    even = is_even() == 1
    coef_ref[0] = 1.0 - DT_TRACER * (jnp.abs(u) + jnp.abs(v))
    coef_ref[1] = -DT_TRACER * lanes(jnp.minimum(u, 0.0), -1)
    coef_ref[2] = DT_TRACER * lanes(jnp.maximum(u, 0.0), 1)
    coef_ref[3] = jnp.where(even, south, north)
    coef_ref[4] = jnp.where(even, north, south)
    for i, m in enumerate(ms):
        for k in range(5):
            wide_ref[k, i] = jnp.broadcast_to(coef_ref[k, pl.ds(row_of(m) + 8, 1), :], (8, C))


def subcycle(states, ms, wide_ref, first):
    done = {}
    for m in ms:
        k = [wide_ref[j, m - first] for j in range(5)]
        done[m] = [
            k[0] * q + k[1] * lanes(q, -1) + k[2] * lanes(q, 1) + (k[3] * above + k[4] * below)
            for q, above, below in zip(states[m], states[m + 1], states[m - 1])
        ]
    return done


def own_rows(x_ref, ms):
    return {m: [x_ref[pl.ds(8 * g * R + row_of(m), 8, stride=R), :] for g in range(S // 8)] for m in ms}


def stored(ref, slot):
    return [ref[slot, pl.ds(8 * g, 8), :] for g in range(S // 8)]


def store(ref, slot, groups):
    for g, q in enumerate(groups):
        ref[slot, pl.ds(8 * g, 8), :] = q


def halo_rows(message_ref, ms, place):
    return {
        m: [message_ref[pl.ds(pl.multiple_of(place(m) * S + 8 * g, 8), 8), :] for g in range(S // 8)] for m in ms
    }


def react_blocks(conc, scale, w_ref, apart):
    hi = conc.astype(BF16)
    lo = (conc - hi.astype(F32)).astype(BF16)
    both = jnp.concatenate([hi, lo, hi, lo], axis=0)
    size = B * (1 + 2 * PAIRS)
    if not apart:
        whole_y = jnp.dot(w_ref[...], both, preferred_element_type=F32)
    for c in range(S // B):
        if apart:
            y = jnp.dot(w_ref[pl.ds(c * size, size), :], both, preferred_element_type=F32)
        else:
            y = whole_y[c * size : (c + 1) * size]
        rate = y[0:B]
        for p in range(PAIRS):
            at = (1 + 2 * p) * B
            rate = rate + y[at : at + B] * y[at + B : at + 2 * B]
        yield conc[c * B : (c + 1) * B] + rate * scale


def react(conc, scale, w_ref):
    return jnp.concatenate(list(react_blocks(conc, scale, w_ref, False)), axis=0)


B = 64
CHUNKS = 4
H = R // 2


def scale_of(scale_ref, ms):
    return jnp.concatenate([scale_ref[pl.ds(row_of(m), 1), :] for m in ms], axis=1)


def whole(ref, slots):
    return jnp.concatenate([ref[i] for i in slots], axis=1)


def new_winds(winds_ref, near_ref, far_ref):
    even = is_even() == 1
    field = []
    for k in range(2):
        near = near_ref[pl.ds(SUBS * S + 8 * k, 8), :]
        far = far_ref[pl.ds(SUBS * S + 8 * k, 8), :]
        field.append(
            jnp.concatenate([jnp.where(even, far, near), winds_ref[k], jnp.where(even, near, far)], axis=0)
        )
    return wind_step(*field)


FAR_FIRST = R - SUBS
SAVED = 2 * (SUBS - 1) + 1


def near_kernel(scale_ref, x_ref, winds_ref, near_ref, w_ref, conc_ref, saved_ref, coef_ref, wide_ref):
    u, v = new_winds(winds_ref, near_ref, near_ref)
    coefficients(u, v, coef_ref, wide_ref, range(1 - SUBS, FAR_FIRST))
    states = own_rows(x_ref, range(FAR_FIRST + 1)) | halo_rows(near_ref, range(-SUBS, 0), near_row)
    for sub in range(SUBS):
        states = subcycle(states, range(1 - SUBS + sub, FAR_FIRST - sub), wide_ref, 1 - SUBS)
        last = FAR_FIRST - sub - 1
        if sub < SUBS - 1:
            store(saved_ref, 2 * sub, states[last - 1])
            store(saved_ref, 2 * sub + 1, states[last])
        else:
            store(saved_ref, 2 * sub, states[last])
    for m in range(H):
        store(conc_ref, m, states[m])
    conc = whole(conc_ref, range(H))
    for _ in range(NEAR_STEPS):
        conc = react(conc, scale_of(scale_ref, range(H)), w_ref)
    for m in range(H):
        conc_ref[m] = conc[:, m * C : (m + 1) * C]


def far_transport(x_ref, far_ref, saved_ref, wide_ref, conc_ref):
    states = own_rows(x_ref, range(FAR_FIRST - 1, R)) | halo_rows(far_ref, range(R, R + SUBS), far_row)
    for sub in range(SUBS):
        first = FAR_FIRST - sub
        states = subcycle(states, range(first, first + H - 1), wide_ref, FAR_FIRST - SUBS + 1)
        if sub < SUBS - 1:
            states[first - 2] = stored(saved_ref, 2 * sub)
            states[first - 1] = stored(saved_ref, 2 * sub + 1)
    store(conc_ref, 0, stored(saved_ref, SAVED - 1))
    for m in range(H + 1, R):
        store(conc_ref, m - H, states[m])


def rest_kernel(
    scale_ref, x_ref, winds_ref, near_ref, far_ref, w_ref, near_conc_ref, saved_ref,
    out_hbm, winds_out_ref, coef_ref, wide_ref, conc_ref, stage_ref, sems,
):
    copies = []

    def put(blocks, slot, high):
        flat_ref = stage_ref.at[slot].reshape(S * H, C)
        for c, block in enumerate(blocks):
            for i in range(H):
                at = is_even() * (H - 1 - 2 * i) + i
                for g in range(c * B // 8, (c + 1) * B // 8):
                    row = 8 * g - c * B
                    flat_ref[pl.ds(8 * g * H + at, 8, stride=H), :] = block[row : row + 8, i * C : (i + 1) * C]
            part = pl.ds(c * B, B)
            rows = pl.ds(pl.multiple_of(high * H, H), H)
            copies.append(pltpu.make_async_copy(stage_ref.at[slot, part], out_hbm.at[part, rows, :], sems.at[slot, c]))
            copies[-1].start()

    u, v = new_winds(winds_ref, near_ref, far_ref)
    winds_out_ref[0] = u[8:24]
    winds_out_ref[1] = v[8:24]
    coefficients(u, v, coef_ref, wide_ref, range(FAR_FIRST - SUBS + 1, R + SUBS - 1))
    conc = whole(near_conc_ref, range(H))
    for step in range(NEAR_STEPS, CHEM_STEPS):
        conc = react(conc, scale_of(scale_ref, range(H)), w_ref)
    put([conc[c * B : (c + 1) * B] for c in range(S // B)], 0, is_even())
    far_transport(x_ref, far_ref, saved_ref, wide_ref, conc_ref)
    conc = whole(conc_ref, range(H))
    scale = scale_of(scale_ref, range(H, R))
    for step in range(CHEM_STEPS - 1):
        conc = react(conc, scale, w_ref)
    put(react_blocks(conc, scale, w_ref, True), 1, 1 - is_even())
    for copy in copies:
        copy.wait()


NEAR_STEPS = 3


def on_device(tracers, winds, linear, loss, left, right, active):
    size = lax.axis_size(AXES)
    near = [(i, i ^ 1) for i in range(size)]
    far = [(i, (i + 1 if i % 2 else i - 1) % size) for i in range(size)]

    vmem = pl.BlockSpec(memory_space=pltpu.VMEM)
    hbm = pl.BlockSpec(memory_space=pltpu.HBM)
    params = pltpu.CompilerParams(vmem_limit_bytes=VMEM_LIMIT)
    message = jax.ShapeDtypeStruct((SUBS * S + 16, C), F32)
    to_near, to_far, x, winds, raw, loss = pl.pallas_call(
        pack_kernel,
        out_shape=[
            message,
            message,
            jax.ShapeDtypeStruct((S * R, C), F32),
            jax.ShapeDtypeStruct((2, R, C), F32),
            jax.ShapeDtypeStruct((1 + 2 * PAIRS, S, S), F32),
            jax.ShapeDtypeStruct((1, S), F32),
        ],
        in_specs=[hbm] * 6,
        out_specs=[vmem] * 6,
        scratch_shapes=[pltpu.SemaphoreType.DMA((CHUNKS + 5,))],
        compiler_params=params,
    )(
        *[
            pltpu.with_memory_space_constraint(a, pltpu.HBM)
            for a in (tracers.reshape(S * R, C), winds, linear, loss.reshape(1, S), left, right)
        ]
    )
    from_near = lax.ppermute(to_near, AXES, near)
    from_far = lax.ppermute(to_far, AXES, far)
    w, scale = pl.pallas_call(
        weights_kernel,
        out_shape=[jax.ShapeDtypeStruct((OUTS, 4 * S), BF16), jax.ShapeDtypeStruct((R, C), F32)],
        in_specs=[pl.BlockSpec(memory_space=pltpu.SMEM), vmem, vmem],
        out_specs=[vmem, vmem],
        compiler_params=params,
    )(active, raw, loss)
    coef = pltpu.VMEM((5, R + 16, C), F32)
    half = jax.ShapeDtypeStruct((H, S, C), F32)
    conc, saved = pl.pallas_call(
        near_kernel,
        out_shape=[half, jax.ShapeDtypeStruct((SAVED, S, C), F32)],
        in_specs=[vmem] * 5,
        out_specs=[vmem] * 2,
        scratch_shapes=[coef, pltpu.VMEM((5, FAR_FIRST + SUBS - 1, 8, C), F32)],
        compiler_params=params,
    )(scale, x, winds, from_near, w)
    return pl.pallas_call(
        rest_kernel,
        out_shape=[jax.ShapeDtypeStruct((S, R, C), F32), jax.ShapeDtypeStruct((2, R, C), F32)],
        in_specs=[vmem] * 8,
        out_specs=[hbm, vmem],
        scratch_shapes=[
            coef,
            pltpu.VMEM((5, H + SUBS - 2, 8, C), F32),
            pltpu.VMEM((H, S, C), F32),
            pltpu.VMEM((2, S, H, C), F32),
            pltpu.SemaphoreType.DMA((2, S // B)),
        ],
        compiler_params=params,
    )(scale, x, winds, from_near, from_far, w, conc, saved)


def solution(mesh):
    grid = P(None, ("tile", "trac"), None)
    return jax.shard_map(
        on_device,
        mesh=mesh,
        in_specs=(grid, grid, P(), P(), P(), P(), P(("tile", "trac"))),
        out_specs=(grid, grid),
        check_vma=False,
    )
```

```python
import jax
import jax.numpy as jnp
from jax import lax
from jax.experimental import pallas as pl
from jax.experimental.pallas import tpu as pltpu
from jax.sharding import PartitionSpec as P

SUBS = 4
CHEM_STEPS = 3
PAIRS = 4
DT_WIND = 0.1
VISCOSITY = 0.2
DT_TRACER = 0.1
DT_CHEM = 0.1

AXES = ("tile", "trac")
S = 128
R = 16
C = 128
OUTS = S * (1 + 2 * PAIRS)
F32 = jnp.float32
BF16 = jnp.bfloat16
VMEM_LIMIT = 48 * 1024 * 1024


def lanes(x, shift):
    return pltpu.roll(x, shift % C, 1)


def rows_rolled(x, shift):
    return pltpu.roll(x, shift % x.shape[0], 0)


def is_even():
    return 1 - lax.axis_index(AXES) % 2


def pack_kernel(
    x_hbm, winds_hbm, linear_hbm, loss_hbm, left_hbm, right_hbm,
    near_ref, far_ref, x_ref, winds_ref, raw_ref, loss_ref, sems,
):
    even = is_even()
    moves = []
    for k in range(CHUNKS):
        part = pl.ds(k * (S * R // CHUNKS), S * R // CHUNKS)
        moves.append((x_hbm.at[part], x_ref.at[part]))
    moves.append((winds_hbm, winds_ref))
    moves.append((left_hbm, raw_ref.at[pl.ds(1, PAIRS)]))
    moves.append((right_hbm, raw_ref.at[pl.ds(1 + PAIRS, PAIRS)]))
    moves.append((linear_hbm, raw_ref.at[0]))
    moves.append((loss_hbm, loss_ref))
    copies = [pltpu.make_async_copy(a, b, sems.at[i]) for i, (a, b) in enumerate(moves)]
    for copy in copies:
        copy.start()
    for k in range(CHUNKS):
        copies[k].wait()
        for ref, side in ((near_ref, even), (far_ref, 1 - even)):
            for r in range(SUBS):
                for g in range(k * S // 8 // CHUNKS, (k + 1) * S // 8 // CHUNKS):
                    at = 8 * g * R + r + side * (R - SUBS)
                    ref[pl.ds(r * S + 8 * g, 8), :] = x_ref[pl.ds(at, 8, stride=R), :]
    copies[CHUNKS].wait()
    for ref, side in ((near_ref, even), (far_ref, 1 - even)):
        for k in range(2):
            ref[pl.ds(SUBS * S + 8 * k, 8), :] = winds_ref[k, pl.ds(pl.multiple_of(side * 8, 8), 8), :]
    for copy in copies[CHUNKS + 1 :]:
        copy.wait()


def weights_kernel(count_ref, raw_ref, loss_ref, w_ref, scale_ref):
    cell = lax.broadcasted_iota(jnp.int32, (R, C), 0) * C + lax.broadcasted_iota(jnp.int32, (R, C), 1)
    scale_ref[...] = jnp.where(cell < count_ref[0], DT_CHEM, 0.0).astype(F32)
    row = lax.broadcasted_iota(jnp.int32, (S, S), 0)
    col = lax.broadcasted_iota(jnp.int32, (S, S), 1)
    diagonal = jnp.where(row == col, jnp.broadcast_to(loss_ref[...], (S, S)), 0.0)
    parts = [raw_ref[0] - diagonal]
    for p in range(PAIRS):
        parts += [raw_ref[1 + p], raw_ref[1 + PAIRS + p]]
    for i, part in enumerate(parts):
        hi = part.astype(BF16)
        lo = (part - hi.astype(F32)).astype(BF16)
        for c in range(S // B):
            rows = pl.ds((c * len(parts) + i) * B, B)
            for k, piece in enumerate((hi, hi, lo, lo)):
                w_ref[rows, pl.ds(k * S, S)] = piece[c * B : (c + 1) * B]


def tendency(u, v):
    out = []
    for f in (u, v):
        east, west, north, south = lanes(f, -1), lanes(f, 1), rows_rolled(f, -1), rows_rolled(f, 1)
        along = (east - west) * 0.5
        across = (north - south) * 0.5
        spread = east + west + north + south - 4.0 * f
        out.append(-(u * along + v * across) + VISCOSITY * spread)
    return out


def wind_step(u, v):
    du, dv = tendency(u, v)
    fu, fv = u + DT_WIND * du, v + DT_WIND * dv
    du, dv = tendency(fu, fv)
    su = 0.75 * u + 0.25 * (fu + DT_WIND * du)
    sv = 0.75 * v + 0.25 * (fv + DT_WIND * dv)
    du, dv = tendency(su, sv)
    return (
        u / 3.0 + 2.0 / 3.0 * (su + DT_WIND * du),
        v / 3.0 + 2.0 / 3.0 * (sv + DT_WIND * dv),
    )


def row_of(m):
    return is_even() * (R - 1 - 2 * m) + m


def near_row(m):
    return is_even() * (-1 - m) + (1 - is_even()) * (m + SUBS)


def far_row(m):
    return is_even() * (R + SUBS - 1 - m) + (1 - is_even()) * (m - R)


def coefficients(u, v, coef_ref, wide_ref, ms):
    north = -DT_TRACER * rows_rolled(jnp.minimum(v, 0.0), -1)
    south = DT_TRACER * rows_rolled(jnp.maximum(v, 0.0), 1)
    even = is_even() == 1
    coef_ref[0] = 1.0 - DT_TRACER * (jnp.abs(u) + jnp.abs(v))
    coef_ref[1] = -DT_TRACER * lanes(jnp.minimum(u, 0.0), -1)
    coef_ref[2] = DT_TRACER * lanes(jnp.maximum(u, 0.0), 1)
    coef_ref[3] = jnp.where(even, south, north)
    coef_ref[4] = jnp.where(even, north, south)
    for i, m in enumerate(ms):
        for k in range(5):
            wide_ref[k, i] = jnp.broadcast_to(coef_ref[k, pl.ds(row_of(m) + 8, 1), :], (8, C))


def subcycle(states, ms, wide_ref, first):
    done = {}
    for m in ms:
        k = [wide_ref[j, m - first] for j in range(5)]
        done[m] = [
            k[0] * q + k[1] * lanes(q, -1) + k[2] * lanes(q, 1) + (k[3] * above + k[4] * below)
            for q, above, below in zip(states[m], states[m + 1], states[m - 1])
        ]
    return done


def own_rows(x_ref, ms):
    return {m: [x_ref[pl.ds(8 * g * R + row_of(m), 8, stride=R), :] for g in range(S // 8)] for m in ms}


def stored(ref, slot):
    return [ref[slot, pl.ds(8 * g, 8), :] for g in range(S // 8)]


def store(ref, slot, groups):
    for g, q in enumerate(groups):
        ref[slot, pl.ds(8 * g, 8), :] = q


def halo_rows(message_ref, ms, place):
    return {
        m: [message_ref[pl.ds(pl.multiple_of(place(m) * S + 8 * g, 8), 8), :] for g in range(S // 8)] for m in ms
    }


def react_blocks(conc, scale, w_ref, apart):
    hi = conc.astype(BF16)
    lo = (conc - hi.astype(F32)).astype(BF16)
    both = jnp.concatenate([hi, lo, hi, lo], axis=0)
    size = B * (1 + 2 * PAIRS)
    if not apart:
        whole_y = jnp.dot(w_ref[...], both, preferred_element_type=F32)
    for c in range(S // B):
        if apart:
            y = jnp.dot(w_ref[pl.ds(c * size, size), :], both, preferred_element_type=F32)
        else:
            y = whole_y[c * size : (c + 1) * size]
        rate = y[0:B]
        for p in range(PAIRS):
            at = (1 + 2 * p) * B
            rate = rate + y[at : at + B] * y[at + B : at + 2 * B]
        yield conc[c * B : (c + 1) * B] + rate * scale


def react(conc, scale, w_ref):
    return jnp.concatenate(list(react_blocks(conc, scale, w_ref, False)), axis=0)


B = 64
CHUNKS = 4
H = R // 2


def scale_of(scale_ref, ms):
    return jnp.concatenate([scale_ref[pl.ds(row_of(m), 1), :] for m in ms], axis=1)


def whole(ref, slots):
    return jnp.concatenate([ref[i] for i in slots], axis=1)


def new_winds(winds_ref, near_ref, far_ref):
    even = is_even() == 1
    field = []
    for k in range(2):
        near = near_ref[pl.ds(SUBS * S + 8 * k, 8), :]
        far = far_ref[pl.ds(SUBS * S + 8 * k, 8), :]
        field.append(
            jnp.concatenate([jnp.where(even, far, near), winds_ref[k], jnp.where(even, near, far)], axis=0)
        )
    return wind_step(*field)


FAR_FIRST = R - SUBS
SAVED = 2 * (SUBS - 1) + 1


def near_kernel(scale_ref, x_ref, winds_ref, near_ref, w_ref, conc_ref, saved_ref, coef_ref, wide_ref):
    u, v = new_winds(winds_ref, near_ref, near_ref)
    coefficients(u, v, coef_ref, wide_ref, range(1 - SUBS, FAR_FIRST))
    states = own_rows(x_ref, range(FAR_FIRST + 1)) | halo_rows(near_ref, range(-SUBS, 0), near_row)
    for sub in range(SUBS):
        states = subcycle(states, range(1 - SUBS + sub, FAR_FIRST - sub), wide_ref, 1 - SUBS)
        last = FAR_FIRST - sub - 1
        if sub < SUBS - 1:
            store(saved_ref, 2 * sub, states[last - 1])
            store(saved_ref, 2 * sub + 1, states[last])
        else:
            store(saved_ref, 2 * sub, states[last])
    for m in range(H):
        store(conc_ref, m, states[m])
    conc = whole(conc_ref, range(H))
    scale = scale_of(scale_ref, range(H))
    for _ in range(CHEM_STEPS - 1):
        conc = react(conc, scale, w_ref)
    if EARLY:
        early = react(conc[:, : EARLY * C], scale[:, : EARLY * C], w_ref)
        conc = jnp.concatenate([early, conc[:, EARLY * C :]], axis=1)
    for m in range(H):
        conc_ref[m] = conc[:, m * C : (m + 1) * C]


def far_transport(x_ref, far_ref, saved_ref, wide_ref, conc_ref):
    states = own_rows(x_ref, range(FAR_FIRST - 1, R)) | halo_rows(far_ref, range(R, R + SUBS), far_row)
    for sub in range(SUBS):
        first = FAR_FIRST - sub
        states = subcycle(states, range(first, first + H - 1), wide_ref, FAR_FIRST - SUBS + 1)
        if sub < SUBS - 1:
            states[first - 2] = stored(saved_ref, 2 * sub)
            states[first - 1] = stored(saved_ref, 2 * sub + 1)
    store(conc_ref, 0, stored(saved_ref, SAVED - 1))
    for m in range(H + 1, R):
        store(conc_ref, m - H, states[m])


def rest_kernel(
    scale_ref, x_ref, winds_ref, near_ref, far_ref, w_ref, near_conc_ref, saved_ref,
    out_hbm, winds_out_ref, coef_ref, wide_ref, conc_ref, stage_ref, sems,
):
    copies = []

    def put(blocks, slot, high):
        flat_ref = stage_ref.at[slot].reshape(S * H, C)
        for c, block in enumerate(blocks):
            for i in range(H):
                at = is_even() * (H - 1 - 2 * i) + i
                for g in range(c * B // 8, (c + 1) * B // 8):
                    row = 8 * g - c * B
                    flat_ref[pl.ds(8 * g * H + at, 8, stride=H), :] = block[row : row + 8, i * C : (i + 1) * C]
            part = pl.ds(c * B, B)
            rows = pl.ds(pl.multiple_of(high * H, H), H)
            copies.append(pltpu.make_async_copy(stage_ref.at[slot, part], out_hbm.at[part, rows, :], sems.at[slot, c]))
            copies[-1].start()

    u, v = new_winds(winds_ref, near_ref, far_ref)
    winds_out_ref[0] = u[8:24]
    winds_out_ref[1] = v[8:24]
    coefficients(u, v, coef_ref, wide_ref, range(FAR_FIRST - SUBS + 1, R + SUBS - 1))
    late = react(whole(near_conc_ref, range(EARLY, H)), scale_of(scale_ref, range(EARLY, H)), w_ref)
    conc = late
    if EARLY:
        conc = jnp.concatenate([whole(near_conc_ref, range(EARLY)), late], axis=1)
    put([conc[c * B : (c + 1) * B] for c in range(S // B)], 0, is_even())
    far_transport(x_ref, far_ref, saved_ref, wide_ref, conc_ref)
    conc = whole(conc_ref, range(H))
    scale = scale_of(scale_ref, range(H, R))
    for step in range(CHEM_STEPS - 1):
        conc = react(conc, scale, w_ref)
    put(react_blocks(conc, scale, w_ref, True), 1, 1 - is_even())
    for copy in copies:
        copy.wait()


EARLY = 4


def on_device(tracers, winds, linear, loss, left, right, active):
    size = lax.axis_size(AXES)
    near = [(i, i ^ 1) for i in range(size)]
    far = [(i, (i + 1 if i % 2 else i - 1) % size) for i in range(size)]

    vmem = pl.BlockSpec(memory_space=pltpu.VMEM)
    hbm = pl.BlockSpec(memory_space=pltpu.HBM)
    params = pltpu.CompilerParams(vmem_limit_bytes=VMEM_LIMIT)
    message = jax.ShapeDtypeStruct((SUBS * S + 16, C), F32)
    to_near, to_far, x, winds, raw, loss = pl.pallas_call(
        pack_kernel,
        out_shape=[
            message,
            message,
            jax.ShapeDtypeStruct((S * R, C), F32),
            jax.ShapeDtypeStruct((2, R, C), F32),
            jax.ShapeDtypeStruct((1 + 2 * PAIRS, S, S), F32),
            jax.ShapeDtypeStruct((1, S), F32),
        ],
        in_specs=[hbm] * 6,
        out_specs=[vmem] * 6,
        scratch_shapes=[pltpu.SemaphoreType.DMA((CHUNKS + 5,))],
        compiler_params=params,
    )(
        *[
            pltpu.with_memory_space_constraint(a, pltpu.HBM)
            for a in (tracers.reshape(S * R, C), winds, linear, loss.reshape(1, S), left, right)
        ]
    )
    from_near = lax.ppermute(to_near, AXES, near)
    from_far = lax.ppermute(to_far, AXES, far)
    w, scale = pl.pallas_call(
        weights_kernel,
        out_shape=[jax.ShapeDtypeStruct((OUTS, 4 * S), BF16), jax.ShapeDtypeStruct((R, C), F32)],
        in_specs=[pl.BlockSpec(memory_space=pltpu.SMEM), vmem, vmem],
        out_specs=[vmem, vmem],
        compiler_params=params,
    )(active, raw, loss)
    coef = pltpu.VMEM((5, R + 16, C), F32)
    half = jax.ShapeDtypeStruct((H, S, C), F32)
    conc, saved = pl.pallas_call(
        near_kernel,
        out_shape=[half, jax.ShapeDtypeStruct((SAVED, S, C), F32)],
        in_specs=[vmem] * 5,
        out_specs=[vmem] * 2,
        scratch_shapes=[coef, pltpu.VMEM((5, FAR_FIRST + SUBS - 1, 8, C), F32)],
        compiler_params=params,
    )(scale, x, winds, from_near, w)
    return pl.pallas_call(
        rest_kernel,
        out_shape=[jax.ShapeDtypeStruct((S, R, C), F32), jax.ShapeDtypeStruct((2, R, C), F32)],
        in_specs=[vmem] * 8,
        out_specs=[hbm, vmem],
        scratch_shapes=[
            coef,
            pltpu.VMEM((5, H + SUBS - 2, 8, C), F32),
            pltpu.VMEM((H, S, C), F32),
            pltpu.VMEM((2, S, H, C), F32),
            pltpu.SemaphoreType.DMA((2, S // B)),
        ],
        compiler_params=params,
    )(scale, x, winds, from_near, from_far, w, conc, saved)


def solution(mesh):
    grid = P(None, ("tile", "trac"), None)
    return jax.shard_map(
        on_device,
        mesh=mesh,
        in_specs=(grid, grid, P(), P(), P(), P(), P(("tile", "trac"))),
        out_specs=(grid, grid),
        check_vma=False,
    )
```

```python
import jax
import jax.numpy as jnp
from jax import lax
from jax.experimental import pallas as pl
from jax.experimental.pallas import tpu as pltpu
from jax.sharding import PartitionSpec as P

SUBS = 4
CHEM_STEPS = 3
PAIRS = 4
DT_WIND = 0.1
VISCOSITY = 0.2
DT_TRACER = 0.1
DT_CHEM = 0.1

AXES = ("tile", "trac")
S = 128
R = 16
C = 128
OUTS = S * (1 + 2 * PAIRS)
F32 = jnp.float32
BF16 = jnp.bfloat16
VMEM_LIMIT = 48 * 1024 * 1024


def lanes(x, shift):
    return pltpu.roll(x, shift % C, 1)


def rows_rolled(x, shift):
    return pltpu.roll(x, shift % x.shape[0], 0)


def is_even():
    return 1 - lax.axis_index(AXES) % 2


def pack_kernel(
    x_hbm, winds_hbm, near_ref, far_ref, x_ref, winds_ref, sems,
):
    even = is_even()
    moves = []
    for k in range(CHUNKS):
        part = pl.ds(k * (S * R // CHUNKS), S * R // CHUNKS)
        moves.append((x_hbm.at[part], x_ref.at[part]))
    moves.append((winds_hbm, winds_ref))
    copies = [pltpu.make_async_copy(a, b, sems.at[i]) for i, (a, b) in enumerate(moves)]
    for copy in copies:
        copy.start()
    for k in range(CHUNKS):
        copies[k].wait()
        for ref, side in ((near_ref, even), (far_ref, 1 - even)):
            for r in range(SUBS):
                for g in range(k * S // 8 // CHUNKS, (k + 1) * S // 8 // CHUNKS):
                    at = 8 * g * R + r + side * (R - SUBS)
                    ref[pl.ds(r * S + 8 * g, 8), :] = x_ref[pl.ds(at, 8, stride=R), :]
    copies[CHUNKS].wait()
    for ref, side in ((near_ref, even), (far_ref, 1 - even)):
        for k in range(2):
            ref[pl.ds(SUBS * S + 8 * k, 8), :] = winds_ref[k, pl.ds(pl.multiple_of(side * 8, 8), 8), :]


def join_weights(raw_ref, loss_ref, w_ref):
    row = lax.broadcasted_iota(jnp.int32, (S, S), 0)
    col = lax.broadcasted_iota(jnp.int32, (S, S), 1)
    diagonal = jnp.where(row == col, jnp.broadcast_to(loss_ref[...], (S, S)), 0.0)
    parts = [raw_ref[0] - diagonal]
    for p in range(PAIRS):
        parts += [raw_ref[1 + p], raw_ref[1 + PAIRS + p]]
    for i, part in enumerate(parts):
        hi = part.astype(BF16)
        lo = (part - hi.astype(F32)).astype(BF16)
        for c in range(S // B):
            rows = pl.ds((c * len(parts) + i) * B, B)
            for k, piece in enumerate((hi, hi, lo, lo)):
                w_ref[rows, pl.ds(k * S, S)] = piece[c * B : (c + 1) * B]


def tendency(u, v):
    out = []
    for f in (u, v):
        east, west, north, south = lanes(f, -1), lanes(f, 1), rows_rolled(f, -1), rows_rolled(f, 1)
        along = (east - west) * 0.5
        across = (north - south) * 0.5
        spread = east + west + north + south - 4.0 * f
        out.append(-(u * along + v * across) + VISCOSITY * spread)
    return out


def wind_step(u, v):
    du, dv = tendency(u, v)
    fu, fv = u + DT_WIND * du, v + DT_WIND * dv
    du, dv = tendency(fu, fv)
    su = 0.75 * u + 0.25 * (fu + DT_WIND * du)
    sv = 0.75 * v + 0.25 * (fv + DT_WIND * dv)
    du, dv = tendency(su, sv)
    return (
        u / 3.0 + 2.0 / 3.0 * (su + DT_WIND * du),
        v / 3.0 + 2.0 / 3.0 * (sv + DT_WIND * dv),
    )


def row_of(m):
    return is_even() * (R - 1 - 2 * m) + m


def near_row(m):
    return is_even() * (-1 - m) + (1 - is_even()) * (m + SUBS)


def far_row(m):
    return is_even() * (R + SUBS - 1 - m) + (1 - is_even()) * (m - R)


def coefficients(u, v, coef_ref, wide_ref, ms):
    north = -DT_TRACER * rows_rolled(jnp.minimum(v, 0.0), -1)
    south = DT_TRACER * rows_rolled(jnp.maximum(v, 0.0), 1)
    even = is_even() == 1
    coef_ref[0] = 1.0 - DT_TRACER * (jnp.abs(u) + jnp.abs(v))
    coef_ref[1] = -DT_TRACER * lanes(jnp.minimum(u, 0.0), -1)
    coef_ref[2] = DT_TRACER * lanes(jnp.maximum(u, 0.0), 1)
    coef_ref[3] = jnp.where(even, south, north)
    coef_ref[4] = jnp.where(even, north, south)
    for i, m in enumerate(ms):
        for k in range(5):
            wide_ref[k, i] = jnp.broadcast_to(coef_ref[k, pl.ds(row_of(m) + 8, 1), :], (8, C))


def subcycle(states, ms, wide_ref, first):
    done = {}
    for m in ms:
        k = [wide_ref[j, m - first] for j in range(5)]
        done[m] = [
            k[0] * q + k[1] * lanes(q, -1) + k[2] * lanes(q, 1) + (k[3] * above + k[4] * below)
            for q, above, below in zip(states[m], states[m + 1], states[m - 1])
        ]
    return done


def own_rows(x_ref, ms):
    return {m: [x_ref[pl.ds(8 * g * R + row_of(m), 8, stride=R), :] for g in range(S // 8)] for m in ms}


def stored(ref, slot):
    return [ref[slot, pl.ds(8 * g, 8), :] for g in range(S // 8)]


def store(ref, slot, groups):
    for g, q in enumerate(groups):
        ref[slot, pl.ds(8 * g, 8), :] = q


def halo_rows(message_ref, ms, place):
    return {
        m: [message_ref[pl.ds(pl.multiple_of(place(m) * S + 8 * g, 8), 8), :] for g in range(S // 8)] for m in ms
    }


def react_blocks(conc, scale, w_ref, apart):
    hi = conc.astype(BF16)
    lo = (conc - hi.astype(F32)).astype(BF16)
    both = jnp.concatenate([hi, lo, hi, lo], axis=0)
    size = B * (1 + 2 * PAIRS)
    if not apart:
        whole_y = jnp.dot(w_ref[...], both, preferred_element_type=F32)
    for c in range(S // B):
        if apart:
            y = jnp.dot(w_ref[pl.ds(c * size, size), :], both, preferred_element_type=F32)
        else:
            y = whole_y[c * size : (c + 1) * size]
        rate = y[0:B]
        for p in range(PAIRS):
            at = (1 + 2 * p) * B
            rate = rate + y[at : at + B] * y[at + B : at + 2 * B]
        yield conc[c * B : (c + 1) * B] + rate * scale


def react(conc, scale, w_ref):
    return jnp.concatenate(list(react_blocks(conc, scale, w_ref, False)), axis=0)


B = 64
CHUNKS = 4
H = R // 2


def scale_of(count_ref, ms):
    col = lax.broadcasted_iota(jnp.int32, (1, C), 1)
    return jnp.concatenate(
        [jnp.where(col + row_of(m) * C < count_ref[0], DT_CHEM, 0.0).astype(F32) for m in ms], axis=1
    )


def whole(ref, slots):
    return jnp.concatenate([ref[i] for i in slots], axis=1)


def new_winds(winds_ref, near_ref, far_ref):
    even = is_even() == 1
    field = []
    for k in range(2):
        near = near_ref[pl.ds(SUBS * S + 8 * k, 8), :]
        far = far_ref[pl.ds(SUBS * S + 8 * k, 8), :]
        field.append(
            jnp.concatenate([jnp.where(even, far, near), winds_ref[k], jnp.where(even, near, far)], axis=0)
        )
    return wind_step(*field)


FAR_FIRST = R - SUBS
SAVED = 2 * (SUBS - 1) + 1


def near_kernel(
    count_ref, x_ref, winds_ref, near_ref, linear_hbm, loss_hbm, left_hbm, right_hbm,
    conc_ref, saved_ref, w_ref, coef_ref, wide_ref, raw_ref, loss_ref, sems,
):
    moves = [
        (left_hbm, raw_ref.at[pl.ds(1, PAIRS)]),
        (right_hbm, raw_ref.at[pl.ds(1 + PAIRS, PAIRS)]),
        (linear_hbm, raw_ref.at[0]),
        (loss_hbm, loss_ref),
    ]
    copies = [pltpu.make_async_copy(a, b, sems.at[i]) for i, (a, b) in enumerate(moves)]
    for copy in copies:
        copy.start()
    u, v = new_winds(winds_ref, near_ref, near_ref)
    coefficients(u, v, coef_ref, wide_ref, range(1 - SUBS, FAR_FIRST))
    states = own_rows(x_ref, range(FAR_FIRST + 1)) | halo_rows(near_ref, range(-SUBS, 0), near_row)
    for sub in range(SUBS):
        states = subcycle(states, range(1 - SUBS + sub, FAR_FIRST - sub), wide_ref, 1 - SUBS)
        last = FAR_FIRST - sub - 1
        if sub < SUBS - 1:
            store(saved_ref, 2 * sub, states[last - 1])
            store(saved_ref, 2 * sub + 1, states[last])
        else:
            store(saved_ref, 2 * sub, states[last])
    for m in range(H):
        store(conc_ref, m, states[m])
    for copy in copies:
        copy.wait()
    join_weights(raw_ref, loss_ref, w_ref)
    conc = whole(conc_ref, range(H))
    scale = scale_of(count_ref, range(H))
    for _ in range(CHEM_STEPS - 1):
        conc = react(conc, scale, w_ref)
    if EARLY:
        early = react(conc[:, : EARLY * C], scale[:, : EARLY * C], w_ref)
        conc = jnp.concatenate([early, conc[:, EARLY * C :]], axis=1)
    for m in range(H):
        conc_ref[m] = conc[:, m * C : (m + 1) * C]


def far_transport(x_ref, far_ref, saved_ref, wide_ref, conc_ref):
    states = own_rows(x_ref, range(FAR_FIRST - 1, R)) | halo_rows(far_ref, range(R, R + SUBS), far_row)
    for sub in range(SUBS):
        first = FAR_FIRST - sub
        states = subcycle(states, range(first, first + H - 1), wide_ref, FAR_FIRST - SUBS + 1)
        if sub < SUBS - 1:
            states[first - 2] = stored(saved_ref, 2 * sub)
            states[first - 1] = stored(saved_ref, 2 * sub + 1)
    store(conc_ref, 0, stored(saved_ref, SAVED - 1))
    for m in range(H + 1, R):
        store(conc_ref, m - H, states[m])


def rest_kernel(
    count_ref, x_ref, winds_ref, near_ref, far_ref, w_ref, near_conc_ref, saved_ref,
    out_hbm, winds_out_ref, coef_ref, wide_ref, conc_ref, stage_ref, sems,
):
    copies = []

    def put(blocks, slot, high):
        flat_ref = stage_ref.at[slot].reshape(S * H, C)
        for c, block in enumerate(blocks):
            for i in range(H):
                at = is_even() * (H - 1 - 2 * i) + i
                for g in range(c * B // 8, (c + 1) * B // 8):
                    row = 8 * g - c * B
                    flat_ref[pl.ds(8 * g * H + at, 8, stride=H), :] = block[row : row + 8, i * C : (i + 1) * C]
            part = pl.ds(c * B, B)
            rows = pl.ds(pl.multiple_of(high * H, H), H)
            copies.append(pltpu.make_async_copy(stage_ref.at[slot, part], out_hbm.at[part, rows, :], sems.at[slot, c]))
            copies[-1].start()

    u, v = new_winds(winds_ref, near_ref, far_ref)
    winds_out_ref[0] = u[8:24]
    winds_out_ref[1] = v[8:24]
    coefficients(u, v, coef_ref, wide_ref, range(FAR_FIRST - SUBS + 1, R + SUBS - 1))
    late = react(whole(near_conc_ref, range(EARLY, H)), scale_of(count_ref, range(EARLY, H)), w_ref)
    conc = late
    if EARLY:
        conc = jnp.concatenate([whole(near_conc_ref, range(EARLY)), late], axis=1)
    put([conc[c * B : (c + 1) * B] for c in range(S // B)], 0, is_even())
    far_transport(x_ref, far_ref, saved_ref, wide_ref, conc_ref)
    conc = whole(conc_ref, range(H))
    scale = scale_of(count_ref, range(H, R))
    for step in range(CHEM_STEPS - 1):
        conc = react(conc, scale, w_ref)
    put(react_blocks(conc, scale, w_ref, True), 1, 1 - is_even())
    for copy in copies:
        copy.wait()


EARLY = 6


def on_device(tracers, winds, linear, loss, left, right, active):
    size = lax.axis_size(AXES)
    near = [(i, i ^ 1) for i in range(size)]
    far = [(i, (i + 1 if i % 2 else i - 1) % size) for i in range(size)]

    vmem = pl.BlockSpec(memory_space=pltpu.VMEM)
    hbm = pl.BlockSpec(memory_space=pltpu.HBM)
    params = pltpu.CompilerParams(vmem_limit_bytes=VMEM_LIMIT)
    message = jax.ShapeDtypeStruct((SUBS * S + 16, C), F32)
    in_hbm = [
        pltpu.with_memory_space_constraint(a, pltpu.HBM)
        for a in (tracers.reshape(S * R, C), winds, linear, loss.reshape(1, S), left, right)
    ]
    to_near, to_far, x, winds = pl.pallas_call(
        pack_kernel,
        out_shape=[message, message, jax.ShapeDtypeStruct((S * R, C), F32), jax.ShapeDtypeStruct((2, R, C), F32)],
        in_specs=[hbm] * 2,
        out_specs=[vmem] * 4,
        scratch_shapes=[pltpu.SemaphoreType.DMA((CHUNKS + 1,))],
        compiler_params=params,
    )(*in_hbm[:2])
    from_near = lax.ppermute(to_near, AXES, near)
    from_far = lax.ppermute(to_far, AXES, far)
    coef = pltpu.VMEM((5, R + 16, C), F32)
    half = jax.ShapeDtypeStruct((H, S, C), F32)
    smem = pl.BlockSpec(memory_space=pltpu.SMEM)
    conc, saved, w = pl.pallas_call(
        near_kernel,
        out_shape=[
            half,
            jax.ShapeDtypeStruct((SAVED, S, C), F32),
            jax.ShapeDtypeStruct((OUTS, 4 * S), BF16),
        ],
        in_specs=[smem] + [vmem] * 3 + [hbm] * 4,
        out_specs=[vmem] * 3,
        scratch_shapes=[
            coef,
            pltpu.VMEM((5, FAR_FIRST + SUBS - 1, 8, C), F32),
            pltpu.VMEM((1 + 2 * PAIRS, S, S), F32),
            pltpu.VMEM((1, S), F32),
            pltpu.SemaphoreType.DMA((4,)),
        ],
        compiler_params=params,
    )(active, x, winds, from_near, *in_hbm[2:])
    return pl.pallas_call(
        rest_kernel,
        out_shape=[jax.ShapeDtypeStruct((S, R, C), F32), jax.ShapeDtypeStruct((2, R, C), F32)],
        in_specs=[smem] + [vmem] * 7,
        out_specs=[hbm, vmem],
        scratch_shapes=[
            coef,
            pltpu.VMEM((5, H + SUBS - 2, 8, C), F32),
            pltpu.VMEM((H, S, C), F32),
            pltpu.VMEM((2, S, H, C), F32),
            pltpu.SemaphoreType.DMA((2, S // B)),
        ],
        compiler_params=params,
    )(active, x, winds, from_near, from_far, w, conc, saved)


def solution(mesh):
    grid = P(None, ("tile", "trac"), None)
    return jax.shard_map(
        on_device,
        mesh=mesh,
        in_specs=(grid, grid, P(), P(), P(), P(), P(("tile", "trac"))),
        out_specs=(grid, grid),
        check_vma=False,
    )
```
